512 devices in a mesh: fsdp: 64 (over y, x, core), tensor: 8 (over z).
Axes of the slice: x: 4, y: 8, z: 8, core: 2. Of those that a mesh axis runs over, the one named last changes fastest.
Arguments:
- gradient: bfloat16 [8192, 28672], P('fsdp', 'tensor')
- momentum: bfloat16 [8192, 28672], P('fsdp', 'tensor')
- q_basis: bfloat16 [256, 28672], P('fsdp', 'tensor'), may hold values from -0.03125 to 0.03125
Outputs:
- momentum_next: bfloat16 [8192, 28672], P('fsdp', 'tensor')
- update: bfloat16 [8192, 28672], P('fsdp', 'tensor')
- q_next: bfloat16 [256, 28672], P('fsdp', 'tensor')
The draws below stay inside these ranges and needn't reach their ends.
All inputs are finite; a program needn't handle non-finite values.
Results may differ from the reference program's by a relative error of at most 0.038.
Values may be sent and summed in bfloat16 or wider, within the bound.
No kernel may reach another device: no remote copies, remote signals or barrier semaphores. Data moves between devices by JAX's collectives and lax.ppermute only.
A program may use at most 64 MiB of HBM per device.

```python
import math
import jax
import jax.numpy as jnp
from jax import lax

D = 8192
FF = 28672
RANK = 256


def shared_parts(key, rise):
    row_key = jax.random.fold_in(key, 0)
    col_key = jax.random.fold_in(key, 1)
    left_key = jax.random.fold_in(key, 3)
    right_key = jax.random.fold_in(key, 4)
    group_key = jax.random.fold_in(key, 5)
    row_scale = jnp.exp(jax.random.uniform(row_key, (D, 1), jnp.float32, math.log(0.3), math.log(3.0)))
    ramp = jnp.exp(math.log(rise) * jnp.arange(FF, dtype=jnp.float32)[None, :] / (FF - 1))
    col_scale = ramp * jnp.exp(jax.random.uniform(col_key, (1, FF), jnp.float32, math.log(0.3), math.log(3.0)))
    left_table = jax.random.normal(left_key, (D, 16), jnp.float32)
    right_factor = jax.random.normal(right_key, (1, FF), jnp.float32)
    column_groups = jax.random.randint(group_key, (FF,), 0, 16)
    structure = left_table[:, column_groups] * (1.7320508 * right_factor)
    return (row_scale, col_scale, structure)


def draw_gradient(key, part):
    rise = 3.0
    row_scale, col_scale, structure = shared_parts(key, rise)
    key = jax.random.fold_in(key, 11)
    noise = jax.random.normal(key, (D, FF), jnp.float32)
    return (row_scale * col_scale * (noise + structure)).astype(jnp.bfloat16)


def draw_momentum(key, part):
    rise = 3.0
    row_scale, col_scale, structure = shared_parts(key, rise)
    key = jax.random.fold_in(key, 12)
    noise = jax.random.normal(key, (D, FF), jnp.float32)
    return (2.0 * row_scale * col_scale * (noise + structure)).astype(jnp.bfloat16)


def level_of(rng, dims, cuts, low, top_value):
    loudness = 1.0
    for dim, parts in cuts:
        steps = jax.random.uniform(jax.random.fold_in(jax.random.fold_in(rng, 6), dim), (parts,), jnp.float32, low / len(cuts), top_value / len(cuts))
        loudness = loudness * jnp.repeat(jnp.exp(steps), dims[dim] // parts).reshape((-1,) + (1,) * (len(dims) - 1 - dim))
    return loudness


def gaussian(rng, extent, deviation, most, cuts=(), kind=jnp.bfloat16):
    drawn = deviation * jax.random.normal(rng, extent, jnp.float32)
    if cuts:
        drawn = drawn * level_of(rng, extent, cuts, -0.22, 0.18)
    return jnp.clip(drawn, -most, most).astype(kind)


def setup_inputs(seed: int = 0) -> dict:
    splits = jax.random.split(jax.random.key(seed), 4)
    return {
        "gradient": draw_gradient(jax.random.fold_in(splits[3], 71), 0),
        "momentum": draw_momentum(jax.random.fold_in(splits[3], 71), 0),
        "q_basis": gaussian(splits[2], (RANK, FF), FF ** -0.5, 0.03125, ((0, 64), (1, 8))),
    }


MU_KEEP = 0.9

def reference(gradient, momentum, q_basis):
    blended = (momentum.astype(jnp.float32) + gradient.astype(jnp.float32)).astype(jnp.bfloat16)
    power_full = lax.dot_general(blended.astype(jnp.float32), q_basis.astype(jnp.float32), (((1,), (1,)), ((), ())), preferred_element_type=jnp.float32)
    gram_total = jnp.dot(power_full.T, power_full, precision=lax.Precision.HIGHEST)
    factor = jnp.linalg.cholesky(gram_total)
    basis = lax.linalg.triangular_solve(factor, power_full, left_side=False, lower=True, transpose_a=True)
    basis_low = basis.astype(jnp.bfloat16)
    project = lax.dot_general(basis_low.astype(jnp.float32), blended.astype(jnp.float32), (((0,), (0,)), ((), ())), preferred_element_type=jnp.float32).astype(jnp.bfloat16)
    project_wide = project.astype(jnp.float32)
    squares = lax.optimization_barrier(jnp.sum(project_wide * project_wide, axis=1, keepdims=True))
    q_next = (project_wide / jnp.sqrt(squares + 1e-06)).astype(jnp.bfloat16)
    carried = jnp.dot(basis_low.astype(jnp.float32), project.astype(jnp.float32), preferred_element_type=jnp.float32)
    momentum_next = (blended.astype(jnp.float32) - (1.0 - MU_KEEP) * carried).astype(jnp.bfloat16)
    scale_factor = math.sqrt(D * FF / RANK)
    update = (scale_factor * jnp.dot(basis_low.astype(jnp.float32), q_next.astype(jnp.float32), preferred_element_type=jnp.float32)).astype(jnp.bfloat16)
    return (momentum_next, update, q_next)
```

```python
import math

import jax
import jax.numpy as jnp
from jax import lax
from jax.sharding import Mesh
from jax.sharding import PartitionSpec as P

D = 8192
FF = 28672
RANK = 256


MU_KEEP = 0.9

NY, NX, NC, NZ = 8, 4, 2, 8


def swap_cores(value):
    return lax.ppermute(value, "c", [(0, 1), (1, 0)])


def gather(value, axis, size):
    spread = jnp.broadcast_to(value[None], (size, *value.shape))
    return lax.all_to_all(spread, axis, 0, 0, tiled=True)


def scatter_sum(value, axis):
    return jnp.sum(lax.all_to_all(value, axis, 0, 0, tiled=True).astype(jnp.float32), axis=0)


def gram_sum(gram):
    part = scatter_sum(gram.reshape(NX * NC, RANK // (NX * NC), RANK), ("x", "c"))
    part = jnp.sum(gather(part, "y", NY), axis=0)
    return gather(part, ("x", "c"), NX * NC).reshape(RANK, RANK)


def halves(value, core):
    half = value.shape[-1] // 2
    first, second = value[..., :half], value[..., half:]
    return jnp.where(core == 0, first, second), jnp.where(core == 0, second, first)


def body(gradient, momentum, q_basis):
    core = lax.axis_index("c")
    rank_dev = q_basis.shape[0]
    blended = (momentum.astype(jnp.float32) + gradient.astype(jnp.float32)).astype(jnp.bfloat16)

    q_half = lax.all_to_all(q_basis, "c", 1, 0, tiled=True)
    q_half = gather(q_half, "y", NY).reshape(-1, q_half.shape[-1])
    q_half = lax.all_gather(q_half, "x", axis=0, tiled=True)
    q_other = swap_cores(q_half)
    b_half, b_other = halves(blended, core)
    contract_last = (((1,), (1,)), ((), ()))
    power_t = lax.dot_general(
        q_half, b_half, contract_last, preferred_element_type=jnp.float32
    ) + lax.dot_general(q_other, b_other, contract_last, preferred_element_type=jnp.float32)
    rows = power_t.shape[1]
    power_t = power_t.reshape(NX, NY, NC * rank_dev, rows).transpose(1, 0, 2, 3)
    power_t = power_t.reshape(RANK, rows).astype(jnp.bfloat16)
    power_t = jnp.sum(gather(power_t, "z", NZ).astype(jnp.float32), axis=0)

    gram = lax.dot_general(
        power_t,
        power_t,
        contract_last,
        precision=lax.Precision.HIGHEST,
        preferred_element_type=jnp.float32,
    )
    factor = jnp.linalg.cholesky(gram_sum(gram))
    basis_t = lax.linalg.triangular_solve(factor, power_t, left_side=True, lower=True)
    basis_t = basis_t.astype(jnp.bfloat16)

    basis_t = basis_t.reshape(NY, NX, NC, rank_dev, rows).transpose(2, 1, 0, 3, 4)
    basis_t = basis_t.reshape(NC, RANK // NC, rows)
    own_t = jnp.where(core == 0, basis_t[0], basis_t[1])
    other_t = jnp.where(core == 0, basis_t[1], basis_t[0])

    contract_rows = (((1,), (0,)), ((), ()))
    other_terms = lax.dot_general(other_t, blended, contract_rows, preferred_element_type=jnp.float32)
    arrived = swap_cores(other_terms.astype(jnp.bfloat16))
    own_terms = lax.dot_general(own_t, blended, contract_rows, preferred_element_type=jnp.float32)
    chip_terms = (own_terms + arrived.astype(jnp.float32)).astype(jnp.bfloat16)
    cols = chip_terms.shape[1]
    project = scatter_sum(chip_terms.reshape(NX * NY, rank_dev, cols), ("x", "y"))
    project = project.astype(jnp.bfloat16)

    own_project = gather(project, "y", NY).reshape(NY * rank_dev, cols)
    own_project = lax.all_gather(own_project, "x", axis=0, tiled=True)
    project_full = jnp.concatenate([own_project, swap_cores(own_project)], axis=0)
    project_wide = project_full.astype(jnp.float32)
    squares = jnp.sum(project_wide * project_wide, axis=1, keepdims=True)
    squares = jnp.sum(gather(squares, "z", NZ), axis=0)
    q_full = (project_wide / jnp.sqrt(squares + 1e-06)).astype(jnp.bfloat16)

    basis_own_first = jnp.concatenate([own_t, other_t], axis=0)
    contract_rank = (((0,), (0,)), ((), ()))
    carried = lax.dot_general(
        basis_own_first, project_full, contract_rank, preferred_element_type=jnp.float32
    )
    momentum_next = (blended.astype(jnp.float32) - (1.0 - MU_KEEP) * carried).astype(jnp.bfloat16)
    scale_factor = math.sqrt(D * FF / RANK)
    scaled = lax.dot_general(
        basis_own_first, q_full, contract_rank, preferred_element_type=jnp.float32
    )
    update = (scale_factor * scaled).astype(jnp.bfloat16)
    place = lax.axis_index("x") * NY + lax.axis_index("y")
    q_next = lax.dynamic_slice_in_dim(q_full, place * rank_dev, rank_dev, 0)
    return (momentum_next, update, q_next)


def solution(mesh):
    split = Mesh(mesh.devices.reshape(NY, NX, NC, NZ), ("y", "x", "c", "z"))
    spec = P(("y", "x", "c"), "z")
    return jax.shard_map(
        body,
        mesh=split,
        in_specs=(spec, spec, spec),
        out_specs=(spec, spec, spec),
        check_vma=False,
    )
```

```python
import math

import jax
import jax.numpy as jnp
from jax import lax
from jax.experimental import pallas as pl
from jax.experimental.pallas import tpu as pltpu
from jax.sharding import Mesh
from jax.sharding import PartitionSpec as P

D = 8192
FF = 28672
RANK = 256


MU_KEEP = 0.9

NY, NX, NC, NZ = 8, 4, 2, 8


def swap_cores(value):
    return lax.ppermute(value, "c", [(0, 1), (1, 0)])


def gather(value, axis, size):
    spread = jnp.broadcast_to(value[None], (size, *value.shape))
    return lax.all_to_all(spread, axis, 0, 0, tiled=True)


def scatter_sum(value, axis):
    return jnp.sum(lax.all_to_all(value, axis, 0, 0, tiled=True).astype(jnp.float32), axis=0)


def gram_sum(power_t):
    half = RANK // 2
    upper, lower = power_t[:half], power_t[half:]

    def product(left, right):
        return lax.dot_general(
            left,
            right,
            (((1,), (1,)), ((), ())),
            precision=lax.Precision.HIGHEST,
            preferred_element_type=jnp.float32,
        )

    gram = jnp.concatenate(
        [product(upper, upper), product(upper, lower), product(lower, lower)], axis=0
    )
    part = scatter_sum(gram.reshape(NX * NC, -1, half), ("x", "c"))
    part = jnp.sum(gather(part, "y", NY), axis=0)
    return gather(part, ("x", "c"), NX * NC).reshape(3 * half, half)


SUB, LANES = 8, 128
PANEL = 64


def across(value, lane):
    return jnp.broadcast_to(value[:, lane : lane + 1], (SUB, LANES))


def down(value, row):
    return jnp.broadcast_to(value[row : row + 1, :], (SUB, LANES))


def eliminate(tiles, base, last):
    first = base // LANES
    groups = PANEL // SUB
    row_id = lax.broadcasted_iota(jnp.int32, (SUB, LANES), 0)
    for top in range(groups):
        lane = (base + top * SUB) % LANES
        cols = [[across(tiles[g, first], lane + k) for g in range(top, groups)] for k in range(SUB)]
        rows = [[down(tiles[top, t], k) for t in range(first, last)] for k in range(SUB)]
        pivots = None
        steps = []
        for k in range(SUB):
            pivot = down(cols[k][0], k)
            inverse = 1.0 / pivot
            pivots = pivot if pivots is None else jnp.where(row_id == k, pivot, pivots)
            step = [c * inverse for c in cols[k]]
            step[0] = jnp.where(row_id > k, step[0], 0.0)
            for m in range(k + 1, SUB):
                entry = down(cols[m][0], k)
                cols[m] = [c - s * entry for c, s in zip(cols[m], step)]
                factor = down(step[0], m)
                rows[m] = [x - factor * y for x, y in zip(rows[m], rows[k])]
            steps.append(step)
        for g in range(top, groups):
            for t in range(first, last):
                value = tiles[g, t]
                for k in range(SUB):
                    value = value - steps[k][g - top] * rows[k][t - first]
                tiles[g, t] = value
        scale = lax.rsqrt(pivots)
        for t in range(first, last):
            tiles[top, t] = tiles[top, t] * scale


def orthonormal_kernel(gram_ref, power_ref, basis_ref, work_ref):
    last = work_ref.shape[1] // LANES
    work_ref[:LANES, :LANES] = gram_ref[:LANES]
    work_ref[:LANES, LANES:RANK] = gram_ref[LANES:RANK]
    work_ref[LANES:, LANES:RANK] = gram_ref[RANK:]
    work_ref[:, RANK:] = power_ref[...]
    for base in range(0, RANK, PANEL):
        first = base // LANES
        tiles = {
            (g, t): work_ref[base + g * SUB : base + (g + 1) * SUB, t * LANES : (t + 1) * LANES]
            for g in range(PANEL // SUB)
            for t in range(first, last)
        }
        eliminate(tiles, base, last)
        for (g, t), tile in tiles.items():
            work_ref[base + g * SUB : base + (g + 1) * SUB, t * LANES : (t + 1) * LANES] = tile
        below = base + PANEL
        if below < RANK:
            start = below // LANES * LANES
            product = lax.dot_general(
                work_ref[base:below, start:RANK],
                work_ref[base:below, start:],
                (((0,), (0,)), ((), ())),
                precision=lax.Precision.HIGHEST,
                preferred_element_type=jnp.float32,
            )
            work_ref[below:, start:] = work_ref[below:, start:] - product[below - start :]
    basis_ref[...] = work_ref[:, RANK:].astype(basis_ref.dtype)


def orthonormal(gram, power_t):
    rows = power_t.shape[1]
    return pl.pallas_call(
        orthonormal_kernel,
        out_shape=jax.ShapeDtypeStruct((RANK, rows), jnp.bfloat16),
        scratch_shapes=[pltpu.VMEM((RANK, RANK + rows), jnp.float32)],
        compiler_params=pltpu.CompilerParams(vmem_limit_bytes=16 * 2**20),
        cost_estimate=pl.CostEstimate(flops=10**9, bytes_accessed=10**6, transcendentals=0),
        name="orthonormal",
    )(gram, power_t)


def finish_kernel(
    first_ref,
    squares_ref,
    basis_ref,
    own_ref,
    other_ref,
    project_ref,
    blended_ref,
    momentum_ref,
    update_ref,
    q_ref,
    left_ref,
):
    inverse = 1.0 / jnp.sqrt(squares_ref[...] + 1e-06)
    rows = momentum_ref.shape[0]

    @pl.when(pl.program_id(0) == 0)
    def _():
        basis = basis_ref[...].astype(jnp.float32).T
        left_ref[:rows] = basis.astype(jnp.bfloat16)
        left_ref[rows:] = (basis * inverse).astype(jnp.bfloat16)

    project = jnp.concatenate([own_ref[...], other_ref[...]], axis=0)
    both = jnp.dot(left_ref[...], project, preferred_element_type=jnp.float32)
    blended = blended_ref[...].astype(jnp.float32)
    momentum_ref[...] = (blended - (1.0 - MU_KEEP) * both[:rows]).astype(jnp.bfloat16)
    update_ref[...] = (math.sqrt(D * FF / RANK) * both[rows:]).astype(jnp.bfloat16)

    shape = (q_ref.shape[0], RANK)
    here = lax.broadcasted_iota(jnp.int32, shape, 1) == first_ref[
        0
    ] + lax.broadcasted_iota(jnp.int32, shape, 0)
    mine = jnp.sum(jnp.where(here, inverse, 0.0), axis=1, keepdims=True)
    q_ref[...] = (project_ref[...].astype(jnp.float32) * mine).astype(jnp.bfloat16)


def finish(first, squares, basis_t, own, other, project, blended):
    rows, cols = blended.shape
    rank_dev = project.shape[0]
    width = 896

    def columns(height):
        return pl.BlockSpec((height, width), lambda j: (0, j))

    def whole(array):
        return pl.BlockSpec(array.shape, lambda j: (0, 0))

    return pl.pallas_call(
        finish_kernel,
        grid=(cols // width,),
        in_specs=[
            pl.BlockSpec(memory_space=pltpu.SMEM),
            whole(squares),
            whole(basis_t),
            columns(RANK // NC),
            columns(RANK // NC),
            columns(rank_dev),
            columns(rows),
        ],
        out_specs=[columns(rows), columns(rows), columns(rank_dev)],
        out_shape=[
            jax.ShapeDtypeStruct((rows, cols), jnp.bfloat16),
            jax.ShapeDtypeStruct((rows, cols), jnp.bfloat16),
            jax.ShapeDtypeStruct((rank_dev, cols), jnp.bfloat16),
        ],
        scratch_shapes=[pltpu.VMEM((2 * rows, RANK), jnp.bfloat16)],
        compiler_params=pltpu.CompilerParams(vmem_limit_bytes=24 * 2**20),
        cost_estimate=pl.CostEstimate(
            flops=4 * rows * RANK * cols, bytes_accessed=5 * 2**20, transcendentals=0
        ),
        name="finish",
    )(first, squares, basis_t, own, other, project, blended)


def own_first(core, rank_dev):
    to = lax.broadcasted_iota(jnp.int32, (RANK, RANK), 0)
    source = lax.broadcasted_iota(jnp.int32, (RANK, RANK), 1)
    i = to % rank_dev
    y = to // rank_dev % NY
    x = to // (rank_dev * NY) % NX
    c = (to // (rank_dev * NY * NX) + core) % NC
    return (((y * NX + x) * NC + c) * rank_dev + i == source).astype(jnp.bfloat16)


def body(gradient, momentum, q_basis):
    core = lax.axis_index("c")
    rank_dev, cols = q_basis.shape
    blended = (momentum.astype(jnp.float32) + gradient.astype(jnp.float32)).astype(jnp.bfloat16)
    order = own_first(core, rank_dev)

    q_own = gather(q_basis, "y", NY).reshape(-1, cols)
    q_own = lax.all_gather(q_own, "x", axis=0, tiled=True)
    q_other = swap_cores(q_own)
    contract_last = (((1,), (1,)), ((), ()))
    power_own = lax.dot_general(q_own, blended, contract_last, preferred_element_type=jnp.float32)
    power_other = lax.dot_general(
        q_other, blended, contract_last, preferred_element_type=jnp.float32
    )
    power_t = jnp.concatenate(
        [power_own.astype(jnp.bfloat16), power_other.astype(jnp.bfloat16)], axis=0
    )
    contract_first = (((0,), (0,)), ((), ()))
    power_t = lax.dot_general(
        order, power_t, contract_first, preferred_element_type=jnp.float32
    ).astype(jnp.bfloat16)
    power_t = jnp.sum(gather(power_t, "z", NZ).astype(jnp.float32), axis=0)

    basis_t = orthonormal(gram_sum(power_t), power_t)
    matmul = (((1,), (0,)), ((), ()))
    basis_t = lax.dot_general(order, basis_t, matmul, preferred_element_type=jnp.float32).astype(
        jnp.bfloat16
    )
    own_t, other_t = basis_t[: RANK // NC], basis_t[RANK // NC :]

    other_terms = lax.dot_general(other_t, blended, matmul, preferred_element_type=jnp.float32)
    arrived = swap_cores(other_terms.astype(jnp.bfloat16))
    own_terms = lax.dot_general(own_t, blended, matmul, preferred_element_type=jnp.float32)
    chip_terms = (own_terms + arrived.astype(jnp.float32)).astype(jnp.bfloat16)
    project = scatter_sum(chip_terms.reshape(NX * NY, rank_dev, cols), ("x", "y"))
    project = project.astype(jnp.bfloat16)

    own_project = gather(project, "y", NY).reshape(NY * rank_dev, cols)
    wide = own_project.astype(jnp.float32)
    squares = gather(jnp.sum(wide * wide, axis=1)[None], ("x", "z"), NX * NZ)
    squares = jnp.sum(squares.reshape(NX, NZ, NY * rank_dev), axis=1).reshape(1, -1)
    own_project = lax.all_gather(own_project, "x", axis=0, tiled=True)
    own_project, squares = lax.optimization_barrier((own_project, squares))
    place = lax.axis_index("x") * NY + lax.axis_index("y")
    return finish(
        (place * rank_dev).reshape(1),
        jnp.concatenate([squares, swap_cores(squares)], axis=1),
        basis_t,
        own_project,
        swap_cores(own_project),
        project,
        blended,
    )


def solution(mesh):
    split = Mesh(mesh.devices.reshape(NY, NX, NC, NZ), ("y", "x", "c", "z"))
    spec = P(("y", "x", "c"), "z")
    return jax.shard_map(
        body,
        mesh=split,
        in_specs=(spec, spec, spec),
        out_specs=(spec, spec, spec),
        check_vma=False,
    )
```

```python
import math

import jax
import jax.numpy as jnp
from jax import lax
from jax.experimental import pallas as pl
from jax.experimental.pallas import tpu as pltpu
from jax.sharding import Mesh
from jax.sharding import PartitionSpec as P

D = 8192
FF = 28672
RANK = 256


MU_KEEP = 0.9

NY, NX, NC, NZ = 8, 4, 2, 8


def swap_cores(value):
    return lax.ppermute(value, "c", [(0, 1), (1, 0)])


def gather(value, axis, size):
    spread = jnp.broadcast_to(value[None], (size, *value.shape))
    return lax.all_to_all(spread, axis, 0, 0, tiled=True)


def scatter_sum(value, axis):
    return jnp.sum(lax.all_to_all(value, axis, 0, 0, tiled=True).astype(jnp.float32), axis=0)


def gram_sum(pieces):
    part = scatter_sum(pieces, "x")
    part = jnp.sum(gather(part, "y", NY), axis=0)
    return gather(part, ("x", "c"), NX * NC).reshape(-1, part.shape[-1])


SUB, LANES = 8, 128
PANEL = 64


def across(value, lane):
    return jnp.broadcast_to(value[:, lane : lane + 1], (SUB, LANES))


def down(value, row):
    return jnp.broadcast_to(value[row : row + 1, :], (SUB, LANES))


def eliminate(tiles, base, last):
    first = base // LANES
    groups = PANEL // SUB
    row_id = lax.broadcasted_iota(jnp.int32, (SUB, LANES), 0)
    for top in range(groups):
        lane = (base + top * SUB) % LANES
        cols = [[across(tiles[g, first], lane + k) for g in range(top, groups)] for k in range(SUB)]
        rows = [[down(tiles[top, t], k) for t in range(first, last)] for k in range(SUB)]
        pivots = None
        steps = []
        for k in range(SUB):
            pivot = down(cols[k][0], k)
            inverse = 1.0 / pivot
            pivots = pivot if pivots is None else jnp.where(row_id == k, pivot, pivots)
            step = [c * inverse for c in cols[k]]
            step[0] = jnp.where(row_id > k, step[0], 0.0)
            for m in range(k + 1, SUB):
                entry = down(cols[m][0], k)
                cols[m] = [c - s * entry for c, s in zip(cols[m], step)]
                factor = down(step[0], m)
                rows[m] = [x - factor * y for x, y in zip(rows[m], rows[k])]
            steps.append(step)
        for g in range(top, groups):
            for t in range(first, last):
                value = tiles[g, t]
                for k in range(SUB):
                    value = value - steps[k][g - top] * rows[k][t - first]
                tiles[g, t] = value
        scale = lax.rsqrt(pivots)
        for t in range(first, last):
            tiles[top, t] = tiles[top, t] * scale


def gram_kernel(core_ref, order_ref, own_ref, other_ref, power_ref, gram_ref):
    half = own_ref.shape[1] // 2
    other = jnp.concatenate([other_ref[:, half:], other_ref[:, :half]], axis=1)
    exact = {"precision": lax.Precision.HIGHEST, "preferred_element_type": jnp.float32}
    power = lax.dot_general(
        order_ref[...].astype(jnp.float32),
        jnp.concatenate([own_ref[...], other], axis=0),
        (((0,), (0,)), ((), ())),
        **exact,
    )
    power_ref[...] = power
    contract_last = (((1,), (1,)), ((), ()))
    upper, lower = power[:LANES], power[LANES:]
    gram = jnp.concatenate(
        [
            lax.dot_general(upper, upper, contract_last, **exact),
            lax.dot_general(upper, lower, contract_last, **exact),
            lax.dot_general(lower, lower, contract_last, **exact),
        ],
        axis=0,
    )
    height = gram_ref.shape[1]
    for x in range(NX):
        even = gram[2 * x * height : (2 * x + 1) * height]
        odd = gram[(2 * x + 1) * height : (2 * x + 2) * height]
        gram_ref[x] = jnp.where(core_ref[0] == 0, even, odd)


def gram_pieces(core, order, own, other):
    rows = own.shape[1]
    vmem = pl.BlockSpec(memory_space=pltpu.VMEM)
    return pl.pallas_call(
        gram_kernel,
        in_specs=[pl.BlockSpec(memory_space=pltpu.SMEM), vmem, vmem, vmem],
        out_specs=[vmem, vmem],
        out_shape=[
            jax.ShapeDtypeStruct((RANK, rows), jnp.float32),
            jax.ShapeDtypeStruct((NX, 3 * LANES // (NX * NC), LANES), jnp.float32),
        ],
        compiler_params=pltpu.CompilerParams(vmem_limit_bytes=16 * 2**20),
        cost_estimate=pl.CostEstimate(flops=10**9, bytes_accessed=10**6, transcendentals=0),
        name="gram_pieces",
    )(core.reshape(1), order, own, other)


def orthonormal_kernel(gram_ref, power_ref, basis_ref, work_ref):
    last = work_ref.shape[1] // LANES
    work_ref[:LANES, :LANES] = gram_ref[:LANES]
    work_ref[:LANES, LANES:RANK] = gram_ref[LANES:RANK]
    work_ref[LANES:, LANES:RANK] = gram_ref[RANK:]
    work_ref[:, RANK:] = power_ref[...]
    for base in range(0, RANK, PANEL):
        first = base // LANES
        tiles = {
            (g, t): work_ref[base + g * SUB : base + (g + 1) * SUB, t * LANES : (t + 1) * LANES]
            for g in range(PANEL // SUB)
            for t in range(first, last)
        }
        eliminate(tiles, base, last)
        for (g, t), tile in tiles.items():
            work_ref[base + g * SUB : base + (g + 1) * SUB, t * LANES : (t + 1) * LANES] = tile
        below = base + PANEL
        if below < RANK:
            start = below // LANES * LANES
            product = lax.dot_general(
                work_ref[base:below, start:RANK],
                work_ref[base:below, start:],
                (((0,), (0,)), ((), ())),
                precision=lax.Precision.HIGHEST,
                preferred_element_type=jnp.float32,
            )
            work_ref[below:, start:] = work_ref[below:, start:] - product[below - start :]
    basis_ref[...] = work_ref[:, RANK:].astype(basis_ref.dtype)


def orthonormal(gram, power_t):
    rows = power_t.shape[1]
    return pl.pallas_call(
        orthonormal_kernel,
        out_shape=jax.ShapeDtypeStruct((RANK, rows), jnp.bfloat16),
        scratch_shapes=[pltpu.VMEM((RANK, RANK + rows), jnp.float32)],
        compiler_params=pltpu.CompilerParams(vmem_limit_bytes=16 * 2**20),
        cost_estimate=pl.CostEstimate(flops=10**9, bytes_accessed=10**6, transcendentals=0),
        name="orthonormal",
    )(gram, power_t)


def terms_kernel(core_ref, basis_ref, blended_ref, other_ref, terms_ref):
    half = RANK // NC
    basis = jnp.where(core_ref[0] == 0, basis_ref[:half], basis_ref[half:])
    both = jnp.concatenate([blended_ref[...], other_ref[...]], axis=0)
    terms = jnp.dot(basis, both, preferred_element_type=jnp.float32)
    terms_ref[0] = terms.astype(jnp.bfloat16)


def project_terms(core, basis_t, blended, other):
    rows, cols = blended.shape
    width = cols // 4
    columns = pl.BlockSpec((rows, width), lambda j: (0, j))
    return pl.pallas_call(
        terms_kernel,
        grid=(4,),
        in_specs=[
            pl.BlockSpec(memory_space=pltpu.SMEM),
            pl.BlockSpec(basis_t.shape, lambda j: (0, 0)),
            columns,
            columns,
        ],
        out_specs=pl.BlockSpec((1, RANK // NC, width), lambda j: (j // 2, 0, j % 2)),
        out_shape=jax.ShapeDtypeStruct((2, RANK // NC, cols // 2), jnp.bfloat16),
        compiler_params=pltpu.CompilerParams(vmem_limit_bytes=24 * 2**20),
        cost_estimate=pl.CostEstimate(
            flops=2 * rows * RANK * cols, bytes_accessed=3 * 2**20, transcendentals=0
        ),
        name="project_terms",
    )(core.reshape(1), basis_t, blended, other)


def finish_kernel(
    core_ref,
    first_ref,
    squares_ref,
    basis_ref,
    own_ref,
    other_ref,
    blended_ref,
    momentum_ref,
    update_ref,
    q_ref,
    left_ref,
    pick_ref,
):
    rows = momentum_ref.shape[0]
    half = RANK // NC
    swap = core_ref[0] != 0

    @pl.when(pl.program_id(0) == 0)
    def _():
        inverse = 1.0 / jnp.sqrt(squares_ref[...] + 1e-06)
        basis = basis_ref[...].astype(jnp.float32).T
        scaled = basis * inverse
        left_ref[:rows] = basis.astype(jnp.bfloat16)
        left_ref[rows:] = scaled.astype(jnp.bfloat16)
        rank = lax.broadcasted_iota(jnp.int32, pick_ref.shape, 1)
        wanted = first_ref[0] + lax.broadcasted_iota(jnp.int32, pick_ref.shape, 0)
        pick_ref[...] = jnp.where(rank == wanted, inverse, 0.0)

    own, other = own_ref[0], other_ref[0]
    project = jnp.concatenate([jnp.where(swap, other, own), jnp.where(swap, own, other)], axis=0)
    both = jnp.dot(left_ref[...], project, preferred_element_type=jnp.float32)
    blended = blended_ref[...].astype(jnp.float32)
    momentum_ref[...] = (blended - (1.0 - MU_KEEP) * both[:rows]).astype(jnp.bfloat16)
    update_ref[...] = (math.sqrt(D * FF / RANK) * both[rows:]).astype(jnp.bfloat16)
    chosen = jnp.where(pick_ref[...] != 0.0, 1.0, 0.0).astype(jnp.bfloat16)
    scale = jnp.sum(pick_ref[...], axis=1, keepdims=True)
    picked = jnp.dot(chosen, project, preferred_element_type=jnp.float32) * scale
    q_ref[...] = picked[: q_ref.shape[0]].astype(jnp.bfloat16)


def finish(core, first, squares, basis_t, own, other, blended, rank_dev):
    rows, cols = blended.shape
    width = cols // 4

    def columns(height):
        return pl.BlockSpec((height, width), lambda j: (0, j))

    halves = pl.BlockSpec((1, RANK // NC, width), lambda j: (j // 2, 0, j % 2))
    smem = pl.BlockSpec(memory_space=pltpu.SMEM)
    return pl.pallas_call(
        finish_kernel,
        grid=(4,),
        in_specs=[
            smem,
            smem,
            pl.BlockSpec(squares.shape, lambda j: (0, 0)),
            pl.BlockSpec((RANK, rows), lambda j: (0, 0)),
            halves,
            halves,
            columns(rows),
        ],
        out_specs=[columns(rows), columns(rows), columns(rank_dev)],
        out_shape=[
            jax.ShapeDtypeStruct((rows, cols), jnp.bfloat16),
            jax.ShapeDtypeStruct((rows, cols), jnp.bfloat16),
            jax.ShapeDtypeStruct((rank_dev, cols), jnp.bfloat16),
        ],
        scratch_shapes=[
            pltpu.VMEM((2 * rows, RANK), jnp.bfloat16),
            pltpu.VMEM((SUB, RANK), jnp.float32),
        ],
        compiler_params=pltpu.CompilerParams(vmem_limit_bytes=24 * 2**20),
        cost_estimate=pl.CostEstimate(
            flops=4 * rows * RANK * cols, bytes_accessed=5 * 2**20, transcendentals=0
        ),
        name="finish",
    )(core.reshape(1), first.reshape(1), squares, basis_t, own, other, blended)


def own_first(core, rank_dev):
    to = lax.broadcasted_iota(jnp.int32, (RANK, RANK), 0)
    source = lax.broadcasted_iota(jnp.int32, (RANK, RANK), 1)
    i = to % rank_dev
    y = to // rank_dev % NY
    x = to // (rank_dev * NY) % NX
    c = (to // (rank_dev * NY * NX) + core) % NC
    return (((y * NX + x) * NC + c) * rank_dev + i == source).astype(jnp.bfloat16)


def body(gradient, momentum, q_basis):
    core, x, y = lax.axis_index("c"), lax.axis_index("x"), lax.axis_index("y")
    rank_dev, cols = q_basis.shape
    half = RANK // NC
    blended = (momentum.astype(jnp.float32) + gradient.astype(jnp.float32)).astype(jnp.bfloat16)
    order = lax.optimization_barrier(own_first(core, rank_dev))

    q_own = gather(q_basis, "y", NY).reshape(-1, cols)
    q_own, blended = lax.optimization_barrier((q_own, blended))
    other = swap_cores(blended)
    q_own = lax.all_gather(q_own, "x", axis=0, tiled=True)
    contract_last = (((1,), (1,)), ((), ()))
    power_own = [
        lax.dot_general(q_own, b, contract_last, preferred_element_type=jnp.float32).astype(
            jnp.bfloat16
        )
        for b in (blended, other)
    ]
    power_own = gather(jnp.concatenate(power_own, axis=1), "z", NZ)
    power_own = jnp.sum(power_own.astype(jnp.float32), axis=0)
    power_t, pieces = gram_pieces(core, order, power_own, swap_cores(power_own))
    basis_t = orthonormal(gram_sum(pieces), power_t)

    terms = project_terms(core, basis_t, blended, other)
    terms = terms.reshape(NX * NY, SUB, cols // 2)
    project = scatter_sum(terms, ("x", "y")).astype(jnp.bfloat16)
    project = gather(project, "y", NY).reshape(NY * SUB, cols // 2)
    wide = project.astype(jnp.float32)
    squares = gather(jnp.sum(wide * wide, axis=1)[None], ("c", "x", "z"), NC * NX * NZ)
    squares = jnp.sum(squares.reshape(NC, 2, NX // 2, NZ, NY * SUB), axis=(1, 3)).reshape(1, RANK)
    project = lax.all_gather(project, "x", axis=0, tiled=True)
    project, squares = lax.optimization_barrier((project, squares))
    project = project.reshape(2, half, cols // 2)
    first = ((y * NX + x) * NC + core) * rank_dev
    return finish(
        core, first, squares, basis_t, project, swap_cores(project), blended, rank_dev
    )


def solution(mesh):
    split = Mesh(mesh.devices.reshape(NY, NX, NC, NZ), ("y", "x", "c", "z"))
    spec = P(("y", "x", "c"), "z")
    return jax.shard_map(
        body,
        mesh=split,
        in_specs=(spec, spec, spec),
        out_specs=(spec, spec, spec),
        check_vma=False,
    )
```

```python
import math

import jax
import jax.numpy as jnp
from jax import lax
from jax.experimental import pallas as pl
from jax.experimental.pallas import tpu as pltpu
from jax.sharding import Mesh
from jax.sharding import PartitionSpec as P

D = 8192
FF = 28672
RANK = 256


MU_KEEP = 0.9

NY, NX, NC, NZ = 8, 4, 2, 8


def swap_cores(value):
    return lax.ppermute(value, "c", [(0, 1), (1, 0)])


def gather(value, axis, size):
    spread = jnp.broadcast_to(value[None], (size, *value.shape))
    return lax.all_to_all(spread, axis, 0, 0, tiled=True)


def scatter_sum(value, axis):
    return jnp.sum(lax.all_to_all(value, axis, 0, 0, tiled=True).astype(jnp.float32), axis=0)


def in_vmem(kernel, name, flops, outs, *args, scalars=0, scratch=(), hbm_outs=0):
    vmem, smem, hbm = (pl.BlockSpec(memory_space=m) for m in (pltpu.VMEM, pltpu.SMEM, pl.ANY))
    return pl.pallas_call(
        kernel,
        in_specs=[smem] * scalars + [vmem] * (len(args) - scalars),
        out_specs=[hbm] * hbm_outs + [vmem] * (len(outs) - hbm_outs),
        out_shape=[jax.ShapeDtypeStruct(shape, dtype) for shape, dtype in outs],
        scratch_shapes=list(scratch),
        compiler_params=pltpu.CompilerParams(vmem_limit_bytes=24 * 2**20),
        cost_estimate=pl.CostEstimate(flops=flops, bytes_accessed=10**6, transcendentals=0),
        name=name,
    )(*args)


def power_kernel(q_ref, blended_ref, other_ref, spread_ref):
    contract_last = (((1,), (1,)), ((), ()))
    power = [
        lax.dot_general(
            q_ref[...], rows[...], contract_last, preferred_element_type=jnp.float32
        ).astype(jnp.bfloat16)
        for rows in (blended_ref, other_ref)
    ]
    power = jnp.concatenate(power, axis=1)
    for z in range(NZ):
        spread_ref[z] = power


def squares_kernel(project_ref, spread_ref):
    wide = project_ref[...].astype(jnp.float32)
    sums = jnp.sum(wide * wide, axis=1, keepdims=True)
    line = jnp.broadcast_to(sums, (sums.shape[0], LANES)).T[:1]
    spread_ref[...] = jnp.broadcast_to(line[None], spread_ref.shape)


def gram_sum(pieces):
    part = scatter_sum(pieces, "x")
    part = jnp.sum(gather(part, "y", NY), axis=0)
    return gather(part, ("x", "c"), NX * NC).reshape(-1, part.shape[-1])


SUB, LANES = 8, 128
PANEL = 64
STEP = 16
BLOCKS = 14


def across(value, lane):
    return jnp.broadcast_to(value[:, lane : lane + 1], (SUB, LANES))


def down(value, row):
    return jnp.broadcast_to(value[row : row + 1, :], (SUB, LANES))


def total(values):
    while len(values) > 1:
        pairs = [values[i] + values[i + 1] for i in range(0, len(values) - 1, 2)]
        values = pairs + values[len(pairs) * 2 :]
    return values[0]


def eliminate(tiles, base, last):
    first = base // LANES
    groups = PANEL // SUB
    depth = STEP // SUB
    row_id = lax.broadcasted_iota(jnp.int32, (SUB, LANES), 0)
    for top in range(0, groups, depth):
        lane = (base + top * SUB) % LANES
        cols = [
            {g: across(tiles[g, first], lane + k) for g in range(top + k // SUB, groups)}
            for k in range(STEP)
        ]
        rows, steps, pivots = [], [], [None] * depth
        for k in range(STEP):
            level, row = divmod(k, SUB)
            here = top + level
            pivot = down(cols[k][here], row)
            inverse = 1.0 / pivot
            known = pivots[level]
            pivots[level] = pivot if known is None else jnp.where(row_id == row, pivot, known)
            step = {g: cols[k][g] * inverse for g in range(here, groups)}
            step[here] = jnp.where(row_id > row, step[here], 0.0)
            for m in range(k + 1, STEP):
                entry = down(cols[k][top + m // SUB], m % SUB)
                for g in cols[m]:
                    cols[m][g] = cols[m][g] - step[g] * entry
            line = {t: down(tiles[here, t], row) for t in range(first, last)}
            for g in range(here, top + depth):
                for t in range(first, last):
                    tiles[g, t] = tiles[g, t] - step[g] * line[t]
            rows.append(line)
            steps.append(step)
        for g in range(top + depth, groups):
            for t in range(first, last):
                tiles[g, t] = tiles[g, t] - total([s[g] * r[t] for s, r in zip(steps, rows)])
        for level in range(depth):
            scale = lax.rsqrt(pivots[level])
            for t in range(first, last):
                tiles[top + level, t] = tiles[top + level, t] * scale


def orthonormal_kernel(
    core_ref, gram_ref, power_ref, blended_ref, other_ref, basis_ref, terms_ref, work_ref
):
    last = work_ref.shape[1] // LANES
    work_ref[:LANES, :LANES] = gram_ref[:LANES]
    work_ref[:LANES, LANES:RANK] = gram_ref[LANES:RANK]
    work_ref[LANES:, LANES:RANK] = gram_ref[RANK:]
    work_ref[:, RANK:] = power_ref[...]
    for base in range(0, RANK, PANEL):
        first = base // LANES
        tiles = {
            (g, t): work_ref[base + g * SUB : base + (g + 1) * SUB, t * LANES : (t + 1) * LANES]
            for g in range(PANEL // SUB)
            for t in range(first, last)
        }
        eliminate(tiles, base, last)
        for (g, t), tile in tiles.items():
            work_ref[base + g * SUB : base + (g + 1) * SUB, t * LANES : (t + 1) * LANES] = tile
        below = base + PANEL
        if below < RANK:
            start = below // LANES * LANES
            product = lax.dot_general(
                work_ref[base:below, start:RANK],
                work_ref[base:below, start:],
                (((0,), (0,)), ((), ())),
                precision=lax.Precision.HIGHEST,
                preferred_element_type=jnp.float32,
            )
            work_ref[below:, start:] = work_ref[below:, start:] - product[below - start :]
    basis_ref[...] = work_ref[:, RANK:].astype(basis_ref.dtype)
    half = RANK // NC
    mine = jnp.where(core_ref[0] == 0, work_ref[:half, RANK:], work_ref[half:, RANK:])
    mine = mine.astype(jnp.bfloat16)
    width = terms_ref.shape[2] // 2
    for j in range(4):
        columns = slice(j * width, (j + 1) * width)
        both = jnp.concatenate([blended_ref[:, columns], other_ref[:, columns]], axis=0)
        terms = jnp.dot(mine, both, preferred_element_type=jnp.float32)
        terms_ref[j // 2, :, j % 2 * width : (j % 2 + 1) * width] = terms.astype(jnp.bfloat16)


def orthonormal(core, gram, power_t, blended, other):
    rows, cols = blended.shape
    vmem = pl.BlockSpec(memory_space=pltpu.VMEM)
    return pl.pallas_call(
        orthonormal_kernel,
        in_specs=[pl.BlockSpec(memory_space=pltpu.SMEM), vmem, vmem, vmem, vmem],
        out_specs=[vmem, vmem],
        out_shape=[
            jax.ShapeDtypeStruct((RANK, NC * rows), jnp.bfloat16),
            jax.ShapeDtypeStruct((2, RANK // NC, cols // 2), jnp.bfloat16),
        ],
        scratch_shapes=[pltpu.VMEM((RANK, RANK + NC * rows), jnp.float32)],
        compiler_params=pltpu.CompilerParams(vmem_limit_bytes=24 * 2**20),
        cost_estimate=pl.CostEstimate(flops=10**9, bytes_accessed=10**6, transcendentals=0),
        name="orthonormal",
    )(core.reshape(1), gram, power_t, blended, other)


def own_first(core, rank_dev):
    def low(value, size):
        return value & (size - 1), value >> (size.bit_length() - 1)

    to = lax.broadcasted_iota(jnp.int32, (RANK, RANK), 0)
    source = lax.broadcasted_iota(jnp.int32, (RANK, RANK), 1)
    i, to = low(to, rank_dev)
    y, to = low(to, NY)
    x, c = low(to, NX)
    c = (c + core) & (NC - 1)
    return (((y * NX + x) * NC + c) * rank_dev + i == source).astype(jnp.float32)


def gram_kernel(core_ref, own_ref, other_ref, power_ref, gram_ref):
    half = own_ref.shape[1] // 2
    other = jnp.concatenate([other_ref[:, half:], other_ref[:, :half]], axis=1)
    exact = {"precision": lax.Precision.HIGHEST, "preferred_element_type": jnp.float32}
    power = lax.dot_general(
        own_first(core_ref[0], RANK // (NY * NX * NC)),
        jnp.concatenate([own_ref[...], other], axis=0),
        (((0,), (0,)), ((), ())),
        **exact,
    )
    power_ref[...] = power
    contract_last = (((1,), (1,)), ((), ()))
    upper, lower = power[:LANES], power[LANES:]
    gram = jnp.concatenate(
        [
            lax.dot_general(upper, upper, contract_last, **exact),
            lax.dot_general(upper, lower, contract_last, **exact),
            lax.dot_general(lower, lower, contract_last, **exact),
        ],
        axis=0,
    )
    height = gram_ref.shape[1]
    for x in range(NX):
        even = gram[2 * x * height : (2 * x + 1) * height]
        odd = gram[(2 * x + 1) * height : (2 * x + 2) * height]
        gram_ref[x] = jnp.where(core_ref[0] == 0, even, odd)


def gram_pieces(core, own, other):
    rows = own.shape[1]
    vmem = pl.BlockSpec(memory_space=pltpu.VMEM)
    return pl.pallas_call(
        gram_kernel,
        in_specs=[pl.BlockSpec(memory_space=pltpu.SMEM), vmem, vmem],
        out_specs=[vmem, vmem],
        out_shape=[
            jax.ShapeDtypeStruct((RANK, rows), jnp.float32),
            jax.ShapeDtypeStruct((NX, 3 * LANES // (NX * NC), LANES), jnp.float32),
        ],
        compiler_params=pltpu.CompilerParams(vmem_limit_bytes=16 * 2**20),
        cost_estimate=pl.CostEstimate(flops=10**9, bytes_accessed=10**6, transcendentals=0),
        name="gram_pieces",
    )(core.reshape(1), own, other)


def prepare_kernel(core_ref, place_ref, squares_ref, basis_ref, left_ref, pick_ref):
    swap = core_ref[0] != 0
    rows = left_ref.shape[0] // 2

    def own_half_first(value):
        first, second = jnp.split(value, 2, 1)
        turned = jnp.concatenate([second, first], axis=1)
        return jnp.where(swap, turned, value)

    inverse = own_half_first(1.0 / jnp.sqrt(squares_ref[...] + 1e-06))
    basis = own_half_first(basis_ref[:, :rows].astype(jnp.float32).T)
    left_ref[:rows] = basis.astype(jnp.bfloat16)
    left_ref[rows:] = (basis * inverse).astype(jnp.bfloat16)
    rank = lax.broadcasted_iota(jnp.int32, pick_ref.shape, 1)
    wanted = place_ref[0] + lax.broadcasted_iota(jnp.int32, pick_ref.shape, 0)
    pick_ref[...] = jnp.where(rank == wanted, inverse, 0.0)


def finish_kernel(
    left_ref,
    pick_ref,
    own_ref,
    other_ref,
    blended_ref,
    momentum_hbm,
    update_hbm,
    q_hbm,
    momentum_ref,
    update_ref,
    q_ref,
    sems,
    q_sem,
):
    rows, cols = blended_ref.shape
    pick = pick_ref[...]
    scale = jnp.sum(pick, axis=1, keepdims=True)
    chosen = jnp.where(pick != 0.0, 1.0, 0.0).astype(jnp.bfloat16)
    blocks = sems.shape[1]
    width = cols // blocks
    copies = []
    for j in range(blocks):
        columns = slice(j * width, (j + 1) * width)
        side, j = divmod(j, blocks // 2)
        there = slice(j * width, (j + 1) * width)
        project = [ref[side, :, there] for ref in (own_ref, other_ref)]
        project = jnp.concatenate(project, axis=0)
        both = jnp.dot(left_ref[...], project, preferred_element_type=jnp.float32)
        blended = blended_ref[:, columns].astype(jnp.float32)
        momentum = blended - (1.0 - MU_KEEP) * both[:rows]
        momentum_ref[:, columns] = momentum.astype(jnp.bfloat16)
        update_ref[:, columns] = (math.sqrt(D * FF / RANK) * both[rows:]).astype(jnp.bfloat16)
        for n, (source, target) in enumerate(
            ((momentum_ref, momentum_hbm), (update_ref, update_hbm))
        ):
            copy = pltpu.make_async_copy(
                source.at[:, columns],
                target.at[:, columns],
                sems.at[n, side * (blocks // 2) + j],
            )
            copy.start()
            copies.append(copy)
        picked = jnp.dot(chosen, project, preferred_element_type=jnp.float32) * scale
        q_ref[:, columns] = picked[: q_ref.shape[0]].astype(jnp.bfloat16)
    copy = pltpu.make_async_copy(q_ref, q_hbm, q_sem)
    copy.start()
    copies.append(copy)
    for copy in copies:
        copy.wait()


def finish(core, place, squares, basis_t, own, other, blended, rank_dev):
    rows, cols = blended.shape
    whole = ((rows, cols), jnp.bfloat16)
    left, pick = in_vmem(
        prepare_kernel,
        "prepare",
        10**5,
        [((2 * rows, RANK), jnp.bfloat16), ((SUB, RANK), jnp.float32)],
        core.reshape(1),
        place.reshape(1),
        squares,
        basis_t,
        scalars=2,
    )
    return in_vmem(
        finish_kernel,
        "finish",
        4 * rows * RANK * cols,
        [whole, whole, ((rank_dev, cols), jnp.bfloat16)],
        left,
        pick,
        own,
        other,
        blended,
        scratch=[
            pltpu.VMEM(*whole),
            pltpu.VMEM(*whole),
            pltpu.VMEM((rank_dev, cols), jnp.bfloat16),
            pltpu.SemaphoreType.DMA((2, BLOCKS)),
            pltpu.SemaphoreType.DMA,
        ],
        hbm_outs=3,
    )


def body(gradient, momentum, q_basis):
    core, x, y = lax.axis_index("c"), lax.axis_index("x"), lax.axis_index("y")
    rank_dev, cols = q_basis.shape
    half = RANK // NC
    blended = (momentum.astype(jnp.float32) + gradient.astype(jnp.float32)).astype(jnp.bfloat16)

    q_own = gather(q_basis, "y", NY).reshape(-1, cols)
    q_own, other = lax.optimization_barrier((q_own, swap_cores(blended)))
    q_own = lax.all_gather(q_own, "x", axis=0, tiled=True)
    rows = NC * blended.shape[0]
    (spread,) = in_vmem(
        power_kernel,
        "power",
        2 * half * rows * cols,
        [((NZ, half, rows), jnp.bfloat16)],
        q_own,
        blended,
        other,
    )
    power_own = jnp.sum(
        lax.all_to_all(spread, "z", 0, 0, tiled=True).astype(jnp.float32), axis=0
    )
    power_t, pieces = gram_pieces(core, power_own, swap_cores(power_own))
    basis_t, terms = orthonormal(core, gram_sum(pieces), power_t, blended, other)

    terms = terms.reshape(NX * NY, SUB, cols // 2)
    project = scatter_sum(terms, ("x", "y")).astype(jnp.bfloat16)
    project = gather(project, "y", NY).reshape(NY * SUB, cols // 2)
    peers = NC * NX * NZ
    (spread,) = in_vmem(
        squares_kernel,
        "squares",
        10**6,
        [((peers, 1, NY * SUB), jnp.float32)],
        project,
    )
    squares = lax.all_to_all(spread, ("c", "x", "z"), 0, 0, tiled=True)
    squares = jnp.sum(squares.reshape(NC, 2, NX // 2, NZ, NY * SUB), axis=(1, 3)).reshape(1, RANK)
    project = lax.all_gather(project, "x", axis=0, tiled=True)
    project, squares = lax.optimization_barrier((project, squares))
    project = project.reshape(2, half, cols // 2)
    place = (((y * NX + x) * NC + core) * rank_dev + RANK - half * core) % RANK
    return finish(
        core, place, squares, basis_t, project, swap_cores(project), blended, rank_dev
    )


def solution(mesh):
    split = Mesh(mesh.devices.reshape(NY, NX, NC, NZ), ("y", "x", "c", "z"))
    spec = P(("y", "x", "c"), "z")
    return jax.shard_map(
        body,
        mesh=split,
        in_specs=(spec, spec, spec),
        out_specs=(spec, spec, spec),
        check_vma=False,
    )
```

```python
import math

import jax
import jax.numpy as jnp
from jax import lax
from jax.experimental import pallas as pl
from jax.experimental.pallas import tpu as pltpu
from jax.sharding import Mesh
from jax.sharding import PartitionSpec as P

D = 8192
FF = 28672
RANK = 256


MU_KEEP = 0.9

NY, NX, NC, NZ = 8, 4, 2, 8


def swap_cores(value):
    return lax.ppermute(value, "c", [(0, 1), (1, 0)])


def gather(value, axis, size):
    spread = jnp.broadcast_to(value[None], (size, *value.shape))
    return lax.all_to_all(spread, axis, 0, 0, tiled=True)


def scatter_sum(value, axis):
    return jnp.sum(lax.all_to_all(value, axis, 0, 0, tiled=True).astype(jnp.float32), axis=0)


def in_vmem(kernel, name, flops, outs, *args, scalars=0, scratch=(), hbm_outs=0):
    vmem, smem, hbm = (pl.BlockSpec(memory_space=m) for m in (pltpu.VMEM, pltpu.SMEM, pl.ANY))
    return pl.pallas_call(
        kernel,
        in_specs=[smem] * scalars + [vmem] * (len(args) - scalars),
        out_specs=[hbm] * hbm_outs + [vmem] * (len(outs) - hbm_outs),
        out_shape=[jax.ShapeDtypeStruct(shape, dtype) for shape, dtype in outs],
        scratch_shapes=list(scratch),
        compiler_params=pltpu.CompilerParams(vmem_limit_bytes=24 * 2**20),
        cost_estimate=pl.CostEstimate(flops=flops, bytes_accessed=10**6, transcendentals=0),
        name=name,
    )(*args)


def power_kernel(q_ref, blended_ref, other_ref, spread_ref):
    contract_last = (((1,), (1,)), ((), ()))
    power = [
        lax.dot_general(
            q_ref[...], rows[...], contract_last, preferred_element_type=jnp.float32
        ).astype(jnp.bfloat16)
        for rows in (blended_ref, other_ref)
    ]
    power = jnp.concatenate(power, axis=1)
    for z in range(NZ):
        spread_ref[z] = power


def squares_kernel(project_ref, spread_ref):
    wide = project_ref[...].astype(jnp.float32)
    sums = jnp.sum(wide * wide, axis=1, keepdims=True)
    line = jnp.broadcast_to(sums, (sums.shape[0], LANES)).T[:1]
    spread_ref[...] = jnp.broadcast_to(line[None], spread_ref.shape)


def gram_sum(pieces):
    part = scatter_sum(pieces, "x")
    part = jnp.sum(gather(part, "y", NY), axis=0)
    return gather(part, ("x", "c"), NX * NC).reshape(-1, part.shape[-1])


SUB, LANES = 8, 128
PANEL = 64
STEP = 16
BLOCKS = 14


def across(value, lane):
    return jnp.broadcast_to(value[:, lane : lane + 1], (SUB, LANES))


def down(value, row):
    return jnp.broadcast_to(value[row : row + 1, :], (SUB, LANES))


def total(values):
    while len(values) > 1:
        pairs = [values[i] + values[i + 1] for i in range(0, len(values) - 1, 2)]
        values = pairs + values[len(pairs) * 2 :]
    return values[0]


def eliminate(tiles, base, last):
    first = base // LANES
    groups = PANEL // SUB
    depth = STEP // SUB
    row_id = lax.broadcasted_iota(jnp.int32, (SUB, LANES), 0)
    for top in range(0, groups, depth):
        lane = (base + top * SUB) % LANES
        cols = [
            {g: across(tiles[g, first], lane + k) for g in range(top + k // SUB, groups)}
            for k in range(STEP)
        ]
        rows, steps, pivots = [], [], [None] * depth
        for k in range(STEP):
            level, row = divmod(k, SUB)
            here = top + level
            pivot = down(cols[k][here], row)
            inverse = 1.0 / pivot
            known = pivots[level]
            pivots[level] = pivot if known is None else jnp.where(row_id == row, pivot, known)
            step = {g: cols[k][g] * inverse for g in range(here, groups)}
            step[here] = jnp.where(row_id > row, step[here], 0.0)
            for m in range(k + 1, STEP):
                entry = down(cols[k][top + m // SUB], m % SUB)
                for g in cols[m]:
                    cols[m][g] = cols[m][g] - step[g] * entry
            line = {t: down(tiles[here, t], row) for t in range(first, last)}
            for g in range(here, top + depth):
                for t in range(first, last):
                    tiles[g, t] = tiles[g, t] - step[g] * line[t]
            rows.append(line)
            steps.append(step)
        for g in range(top + depth, groups):
            for t in range(first, last):
                tiles[g, t] = tiles[g, t] - total([s[g] * r[t] for s, r in zip(steps, rows)])
        for level in range(depth):
            scale = lax.rsqrt(pivots[level])
            for t in range(first, last):
                tiles[top + level, t] = tiles[top + level, t] * scale


def own_ranks(core, height):
    j = lax.broadcasted_iota(jnp.int32, (height, RANK), 0)
    source = lax.broadcasted_iota(jnp.int32, (height, RANK), 1)
    size = RANK // (NY * NX * NC)
    c = jnp.where(j < RANK // NC, core, 1 - core)
    j = j & (RANK // NC - 1)
    low = j & (size - 1)
    return ((j - low) * NC + c * size + low == source).astype(jnp.bfloat16)


def orthonormal_kernel(
    core_ref, gram_ref, power_ref, blended_ref, other_ref, basis_ref, terms_ref, work_ref
):
    last = work_ref.shape[1] // LANES
    work_ref[:LANES, :LANES] = gram_ref[:LANES]
    work_ref[:LANES, LANES:RANK] = gram_ref[LANES:RANK]
    work_ref[LANES:, LANES:RANK] = gram_ref[RANK:]
    work_ref[:, RANK:] = power_ref[...]
    for base in range(0, RANK, PANEL):
        first = base // LANES
        tiles = {
            (g, t): work_ref[base + g * SUB : base + (g + 1) * SUB, t * LANES : (t + 1) * LANES]
            for g in range(PANEL // SUB)
            for t in range(first, last)
        }
        eliminate(tiles, base, last)
        for (g, t), tile in tiles.items():
            work_ref[base + g * SUB : base + (g + 1) * SUB, t * LANES : (t + 1) * LANES] = tile
        below = base + PANEL
        if below < RANK:
            start = below // LANES * LANES
            product = lax.dot_general(
                work_ref[base:below, start:RANK],
                work_ref[base:below, start:],
                (((0,), (0,)), ((), ())),
                precision=lax.Precision.HIGHEST,
                preferred_element_type=jnp.float32,
            )
            work_ref[below:, start:] = work_ref[below:, start:] - product[below - start :]
    basis_ref[...] = work_ref[:, RANK:].astype(basis_ref.dtype)
    mine = jnp.dot(
        own_ranks(core_ref[0], RANK // NC), basis_ref[...], preferred_element_type=jnp.float32
    )
    mine = mine.astype(jnp.bfloat16)
    width = terms_ref.shape[2] // 2
    for j in range(4):
        columns = slice(j * width, (j + 1) * width)
        both = jnp.concatenate([blended_ref[:, columns], other_ref[:, columns]], axis=0)
        terms = jnp.dot(mine, both, preferred_element_type=jnp.float32)
        terms_ref[j // 2, :, j % 2 * width : (j % 2 + 1) * width] = terms.astype(jnp.bfloat16)


def orthonormal(core, gram, power_t, blended, other):
    rows, cols = blended.shape
    vmem = pl.BlockSpec(memory_space=pltpu.VMEM)
    return pl.pallas_call(
        orthonormal_kernel,
        in_specs=[pl.BlockSpec(memory_space=pltpu.SMEM), vmem, vmem, vmem, vmem],
        out_specs=[vmem, vmem],
        out_shape=[
            jax.ShapeDtypeStruct((RANK, NC * rows), jnp.bfloat16),
            jax.ShapeDtypeStruct((2, RANK // NC, cols // 2), jnp.bfloat16),
        ],
        scratch_shapes=[pltpu.VMEM((RANK, RANK + NC * rows), jnp.float32)],
        compiler_params=pltpu.CompilerParams(vmem_limit_bytes=24 * 2**20),
        cost_estimate=pl.CostEstimate(flops=10**9, bytes_accessed=10**6, transcendentals=0),
        name="orthonormal",
    )(core.reshape(1), gram, power_t, blended, other)


def own_first(core, rank_dev):
    def low(value, size):
        return value & (size - 1), value >> (size.bit_length() - 1)

    to = lax.broadcasted_iota(jnp.int32, (RANK, RANK), 0)
    source = lax.broadcasted_iota(jnp.int32, (RANK, RANK), 1)
    i, to = low(to, rank_dev)
    y, to = low(to, NY)
    x, c = low(to, NX)
    c = (c + core) & (NC - 1)
    return (((y * NX + x) * NC + c) * rank_dev + i == source).astype(jnp.float32)


def gram_kernel(core_ref, own_ref, other_ref, power_ref, gram_ref):
    half = own_ref.shape[1] // 2
    other = jnp.concatenate([other_ref[:, half:], other_ref[:, :half]], axis=1)
    exact = {"precision": lax.Precision.HIGHEST, "preferred_element_type": jnp.float32}
    power = lax.dot_general(
        own_first(core_ref[0], RANK // (NY * NX * NC)),
        jnp.concatenate([own_ref[...], other], axis=0),
        (((0,), (0,)), ((), ())),
        **exact,
    )
    power_ref[...] = power
    contract_last = (((1,), (1,)), ((), ()))
    upper, lower = power[:LANES], power[LANES:]
    gram = jnp.concatenate(
        [
            lax.dot_general(upper, upper, contract_last, **exact),
            lax.dot_general(upper, lower, contract_last, **exact),
            lax.dot_general(lower, lower, contract_last, **exact),
        ],
        axis=0,
    )
    height = gram_ref.shape[1]
    for x in range(NX):
        even = gram[2 * x * height : (2 * x + 1) * height]
        odd = gram[(2 * x + 1) * height : (2 * x + 2) * height]
        gram_ref[x] = jnp.where(core_ref[0] == 0, even, odd)


def gram_pieces(core, own, other):
    rows = own.shape[1]
    vmem = pl.BlockSpec(memory_space=pltpu.VMEM)
    return pl.pallas_call(
        gram_kernel,
        in_specs=[pl.BlockSpec(memory_space=pltpu.SMEM), vmem, vmem],
        out_specs=[vmem, vmem],
        out_shape=[
            jax.ShapeDtypeStruct((RANK, rows), jnp.float32),
            jax.ShapeDtypeStruct((NX, 3 * LANES // (NX * NC), LANES), jnp.float32),
        ],
        compiler_params=pltpu.CompilerParams(vmem_limit_bytes=16 * 2**20),
        cost_estimate=pl.CostEstimate(flops=10**9, bytes_accessed=10**6, transcendentals=0),
        name="gram_pieces",
    )(core.reshape(1), own, other)


def prepare_kernel(core_ref, place_ref, squares_ref, basis_ref, own_ref, left_ref, q_ref):
    rows = left_ref.shape[0] // 2
    half = RANK // NC
    inverse = 1.0 / jnp.sqrt(squares_ref[...] + 1e-06)
    turned = jnp.concatenate([inverse[:, half:], inverse[:, :half]], axis=1)
    inverse = jnp.where(core_ref[0] == 0, inverse, turned)
    basis = jnp.dot(
        own_ranks(core_ref[0], RANK), basis_ref[:, :rows], preferred_element_type=jnp.float32
    ).T
    left_ref[:rows] = basis.astype(jnp.bfloat16)
    left_ref[rows:] = (basis * inverse).astype(jnp.bfloat16)
    rank = lax.broadcasted_iota(jnp.int32, (SUB, half), 1)
    chosen = rank == place_ref[0] + lax.broadcasted_iota(jnp.int32, (SUB, half), 0)
    scale = jnp.sum(jnp.where(chosen, inverse[:, :half], 0.0), axis=1, keepdims=True)
    chosen = jnp.where(chosen, 1.0, 0.0).astype(jnp.bfloat16)
    width = own_ref.shape[2]
    for side in range(2):
        picked = jnp.dot(chosen, own_ref[side], preferred_element_type=jnp.float32) * scale
        columns = slice(side * width, (side + 1) * width)
        q_ref[:, columns] = picked[: q_ref.shape[0]].astype(jnp.bfloat16)


def finish_kernel(
    left_ref,
    own_ref,
    other_ref,
    blended_ref,
    momentum_hbm,
    update_hbm,
    momentum_ref,
    update_ref,
    sems,
):
    rows, cols = blended_ref.shape
    blocks = sems.shape[1]
    width = cols // blocks
    copies = []
    for j in range(blocks):
        columns = slice(j * width, (j + 1) * width)
        side, k = divmod(j, blocks // 2)
        there = slice(k * width, (k + 1) * width)
        project = [ref[side, :, there] for ref in (own_ref, other_ref)]
        project = jnp.concatenate(project, axis=0)
        both = jnp.dot(left_ref[...], project, preferred_element_type=jnp.float32)
        blended = blended_ref[:, columns].astype(jnp.float32)
        momentum = blended - (1.0 - MU_KEEP) * both[:rows]
        momentum_ref[:, columns] = momentum.astype(jnp.bfloat16)
        update_ref[:, columns] = (math.sqrt(D * FF / RANK) * both[rows:]).astype(jnp.bfloat16)
        for n, (source, target) in enumerate(
            ((momentum_ref, momentum_hbm), (update_ref, update_hbm))
        ):
            copy = pltpu.make_async_copy(
                source.at[:, columns], target.at[:, columns], sems.at[n, j]
            )
            copy.start()
            copies.append(copy)
    for copy in copies:
        copy.wait()


def finish(core, place, squares, basis_t, own, other, blended, rank_dev):
    rows, cols = blended.shape
    whole = ((rows, cols), jnp.bfloat16)
    left, q_next = in_vmem(
        prepare_kernel,
        "prepare",
        10**5,
        [((2 * rows, RANK), jnp.bfloat16), ((rank_dev, cols), jnp.bfloat16)],
        core.reshape(1),
        place.reshape(1),
        squares,
        basis_t,
        own,
        scalars=2,
    )
    momentum_next, update = in_vmem(
        finish_kernel,
        "finish",
        4 * rows * RANK * cols,
        [whole, whole],
        left,
        own,
        other,
        blended,
        scratch=[pltpu.VMEM(*whole), pltpu.VMEM(*whole), pltpu.SemaphoreType.DMA((2, BLOCKS))],
        hbm_outs=2,
    )
    return momentum_next, update, q_next


def body(gradient, momentum, q_basis):
    core, x, y = lax.axis_index("c"), lax.axis_index("x"), lax.axis_index("y")
    rank_dev, cols = q_basis.shape
    half = RANK // NC
    blended = (momentum.astype(jnp.float32) + gradient.astype(jnp.float32)).astype(jnp.bfloat16)

    q_own = gather(q_basis, "y", NY).reshape(-1, cols)
    q_own, other = lax.optimization_barrier((q_own, swap_cores(blended)))
    q_own = lax.all_gather(q_own, "x", axis=0, tiled=True)
    rows = NC * blended.shape[0]
    (spread,) = in_vmem(
        power_kernel,
        "power",
        2 * half * rows * cols,
        [((NZ, half, rows), jnp.bfloat16)],
        q_own,
        blended,
        other,
    )
    power_own = jnp.sum(
        lax.all_to_all(spread, "z", 0, 0, tiled=True).astype(jnp.float32), axis=0
    )
    power_t, pieces = gram_pieces(core, power_own, swap_cores(power_own))
    basis_t, terms = orthonormal(core, gram_sum(pieces), power_t, blended, other)

    terms = terms.reshape(NX, NY * SUB, cols // 2)
    project = scatter_sum(terms, "x").astype(jnp.bfloat16).reshape(NY, SUB, cols // 2)
    project = scatter_sum(project, "y").astype(jnp.bfloat16)
    project = gather(project, "y", NY).reshape(NY * SUB, cols // 2)
    peers = NC * NX * NZ
    (spread,) = in_vmem(
        squares_kernel,
        "squares",
        10**6,
        [((peers, 1, NY * SUB), jnp.float32)],
        project,
    )
    squares = lax.all_to_all(spread, ("c", "x", "z"), 0, 0, tiled=True)
    squares = jnp.sum(squares.reshape(NC, 2, NX // 2, NZ, NY * SUB), axis=(1, 3)).reshape(1, RANK)
    project = lax.all_gather(project, "x", axis=0, tiled=True)
    project, squares = lax.optimization_barrier((project, squares))
    project = project.reshape(2, half, cols // 2)
    place = (y * NX + x) * rank_dev
    return finish(
        core, place, squares, basis_t, project, swap_cores(project), blended, rank_dev
    )


def solution(mesh):
    split = Mesh(mesh.devices.reshape(NY, NX, NC, NZ), ("y", "x", "c", "z"))
    spec = P(("y", "x", "c"), "z")
    return jax.shard_map(
        body,
        mesh=split,
        in_specs=(spec, spec, spec),
        out_specs=(spec, spec, spec),
        check_vma=False,
    )
```

```python
import math

import jax
import jax.numpy as jnp
from jax import lax
from jax.experimental import pallas as pl
from jax.experimental.pallas import tpu as pltpu
from jax.sharding import Mesh
from jax.sharding import PartitionSpec as P

D = 8192
FF = 28672
RANK = 256


MU_KEEP = 0.9

NY, NX, NC, NZ = 8, 4, 2, 8


def swap_cores(value):
    return lax.ppermute(value, "c", [(0, 1), (1, 0)])


def gather(value, axis, size):
    spread = jnp.broadcast_to(value[None], (size, *value.shape))
    return lax.all_to_all(spread, axis, 0, 0, tiled=True)


def scatter_sum(value, axis):
    return jnp.sum(lax.all_to_all(value, axis, 0, 0, tiled=True).astype(jnp.float32), axis=0)


def in_vmem(kernel, name, flops, outs, *args, scalars=0, scratch=(), hbm_outs=0):
    vmem, smem, hbm = (pl.BlockSpec(memory_space=m) for m in (pltpu.VMEM, pltpu.SMEM, pl.ANY))
    return pl.pallas_call(
        kernel,
        in_specs=[smem] * scalars + [vmem] * (len(args) - scalars),
        out_specs=[hbm] * hbm_outs + [vmem] * (len(outs) - hbm_outs),
        out_shape=[jax.ShapeDtypeStruct(shape, dtype) for shape, dtype in outs],
        scratch_shapes=list(scratch),
        compiler_params=pltpu.CompilerParams(vmem_limit_bytes=24 * 2**20),
        cost_estimate=pl.CostEstimate(flops=flops, bytes_accessed=10**6, transcendentals=0),
        name=name,
    )(*args)


def power_kernel(q_ref, blended_ref, other_ref, spread_ref):
    contract_last = (((1,), (1,)), ((), ()))
    power = [
        lax.dot_general(
            q_ref[...], rows[...], contract_last, preferred_element_type=jnp.float32
        ).astype(jnp.bfloat16)
        for rows in (blended_ref, other_ref)
    ]
    power = jnp.concatenate(power, axis=1)
    for z in range(NZ):
        spread_ref[z] = power


def squares_kernel(project_ref, spread_ref):
    wide = project_ref[...].astype(jnp.float32)
    sums = jnp.sum(wide * wide, axis=1, keepdims=True)
    line = jnp.broadcast_to(sums, (sums.shape[0], LANES)).T[:1]
    spread_ref[...] = jnp.broadcast_to(line[None], spread_ref.shape)


def gram_sum(pieces):
    part = scatter_sum(pieces, "x")
    part = jnp.sum(gather(part, "y", NY), axis=0)
    return gather(part, ("c", "x"), NX * NC).reshape(-1, part.shape[-1])


SUB, LANES = 8, 128
PANEL = 64
STEP = 16
BLOCKS = 14


def across(value, lane):
    return jnp.broadcast_to(value[:, lane : lane + 1], (SUB, LANES))


def down(value, row):
    return jnp.broadcast_to(value[row : row + 1, :], (SUB, LANES))


def total(values):
    while len(values) > 1:
        pairs = [values[i] + values[i + 1] for i in range(0, len(values) - 1, 2)]
        values = pairs + values[len(pairs) * 2 :]
    return values[0]


def eliminate(tiles, base, last):
    first = base // LANES
    groups = PANEL // SUB
    depth = STEP // SUB
    row_id = lax.broadcasted_iota(jnp.int32, (SUB, LANES), 0)
    for top in range(0, groups, depth):
        lane = (base + top * SUB) % LANES
        cols = [
            {g: across(tiles[g, first], lane + k) for g in range(top + k // SUB, groups)}
            for k in range(STEP)
        ]
        rows, steps, pivots = [], [], [None] * depth
        for k in range(STEP):
            level, row = divmod(k, SUB)
            here = top + level
            pivot = down(cols[k][here], row)
            inverse = 1.0 / pivot
            known = pivots[level]
            pivots[level] = pivot if known is None else jnp.where(row_id == row, pivot, known)
            step = {g: cols[k][g] * inverse for g in range(here, groups)}
            step[here] = jnp.where(row_id > row, step[here], 0.0)
            for m in range(k + 1, STEP):
                entry = down(cols[k][top + m // SUB], m % SUB)
                for g in cols[m]:
                    cols[m][g] = cols[m][g] - step[g] * entry
            line = {t: down(tiles[here, t], row) for t in range(first, last)}
            for g in range(here, top + depth):
                for t in range(first, last):
                    tiles[g, t] = tiles[g, t] - step[g] * line[t]
            rows.append(line)
            steps.append(step)
        for g in range(top + depth, groups):
            for t in range(first, last):
                tiles[g, t] = tiles[g, t] - total([s[g] * r[t] for s, r in zip(steps, rows)])
        for level in range(depth):
            scale = lax.rsqrt(pivots[level])
            for t in range(first, last):
                tiles[top + level, t] = tiles[top + level, t] * scale


def own_ranks(core, height):
    j = lax.broadcasted_iota(jnp.int32, (height, RANK), 0)
    source = lax.broadcasted_iota(jnp.int32, (height, RANK), 1)
    size = RANK // (NY * NX * NC)
    c = jnp.where(j < RANK // NC, core, 1 - core)
    j = j & (RANK // NC - 1)
    low = j & (size - 1)
    return ((j - low) * NC + c * size + low == source).astype(jnp.bfloat16)


def orthonormal_kernel(
    core_ref, gram_ref, power_ref, blended_ref, other_ref, basis_ref, terms_ref, work_ref
):
    last = work_ref.shape[1] // LANES
    half, core = LANES // 2, LANES * 3 // 2
    work_ref[:LANES, :LANES] = gram_ref[:LANES]
    work_ref[:half, LANES:RANK] = gram_ref[LANES:core]
    work_ref[half:LANES, LANES:RANK] = gram_ref[core + LANES :]
    work_ref[LANES:, LANES:RANK] = gram_ref[core : core + LANES]
    work_ref[:, RANK:] = power_ref[...]
    for base in range(0, RANK, PANEL):
        first = base // LANES
        tiles = {
            (g, t): work_ref[base + g * SUB : base + (g + 1) * SUB, t * LANES : (t + 1) * LANES]
            for g in range(PANEL // SUB)
            for t in range(first, last)
        }
        eliminate(tiles, base, last)
        for (g, t), tile in tiles.items():
            work_ref[base + g * SUB : base + (g + 1) * SUB, t * LANES : (t + 1) * LANES] = tile
        below = base + PANEL
        if below < RANK:
            start = below // LANES * LANES
            product = lax.dot_general(
                work_ref[base:below, start:RANK],
                work_ref[base:below, start:],
                (((0,), (0,)), ((), ())),
                precision=lax.Precision.HIGHEST,
                preferred_element_type=jnp.float32,
            )
            work_ref[below:, start:] = work_ref[below:, start:] - product[below - start :]
    basis_ref[...] = work_ref[:, RANK:].astype(basis_ref.dtype)
    mine = jnp.dot(
        own_ranks(core_ref[0], RANK // NC), basis_ref[...], preferred_element_type=jnp.float32
    )
    mine = mine.astype(jnp.bfloat16)
    width = terms_ref.shape[2] // 2
    for j in range(4):
        columns = slice(j * width, (j + 1) * width)
        both = jnp.concatenate([blended_ref[:, columns], other_ref[:, columns]], axis=0)
        terms = jnp.dot(mine, both, preferred_element_type=jnp.float32)
        terms_ref[j // 2, :, j % 2 * width : (j % 2 + 1) * width] = terms.astype(jnp.bfloat16)


def orthonormal(core, gram, power_t, blended, other):
    rows, cols = blended.shape
    vmem = pl.BlockSpec(memory_space=pltpu.VMEM)
    return pl.pallas_call(
        orthonormal_kernel,
        in_specs=[pl.BlockSpec(memory_space=pltpu.SMEM), vmem, vmem, vmem, vmem],
        out_specs=[vmem, vmem],
        out_shape=[
            jax.ShapeDtypeStruct((RANK, NC * rows), jnp.bfloat16),
            jax.ShapeDtypeStruct((2, RANK // NC, cols // 2), jnp.bfloat16),
        ],
        scratch_shapes=[pltpu.VMEM((RANK, RANK + NC * rows), jnp.float32)],
        compiler_params=pltpu.CompilerParams(vmem_limit_bytes=24 * 2**20),
        cost_estimate=pl.CostEstimate(flops=10**9, bytes_accessed=10**6, transcendentals=0),
        name="orthonormal",
    )(core.reshape(1), gram, power_t, blended, other)


def own_first(core, rank_dev):
    def low(value, size):
        return value & (size - 1), value >> (size.bit_length() - 1)

    to = lax.broadcasted_iota(jnp.int32, (RANK, RANK), 0)
    source = lax.broadcasted_iota(jnp.int32, (RANK, RANK), 1)
    i, to = low(to, rank_dev)
    y, to = low(to, NY)
    x, c = low(to, NX)
    c = (c + core) & (NC - 1)
    return (((y * NX + x) * NC + c) * rank_dev + i == source).astype(jnp.float32)


def gram_kernel(core_ref, own_ref, other_ref, power_ref, gram_ref):
    half = own_ref.shape[1] // 2
    other = jnp.concatenate([other_ref[:, half:], other_ref[:, :half]], axis=1)
    exact = {"precision": lax.Precision.HIGHEST, "preferred_element_type": jnp.float32}
    power = lax.dot_general(
        own_first(core_ref[0], RANK // (NY * NX * NC)),
        jnp.concatenate([own_ref[...], other], axis=0),
        (((0,), (0,)), ((), ())),
        **exact,
    )
    power_ref[...] = power
    first = core_ref[0] == 0
    upper, lower = power[:LANES], power[LANES:]
    own = jnp.where(first, upper, lower)
    cross = jnp.where(first, upper[: LANES // 2], upper[LANES // 2 :])
    contract_last = (((1,), (1,)), ((), ()))
    gram = jnp.concatenate(
        [
            lax.dot_general(own, own, contract_last, **exact),
            lax.dot_general(cross, lower, contract_last, **exact),
        ],
        axis=0,
    )
    height = gram_ref.shape[1]
    for x in range(NX):
        gram_ref[x] = gram[x * height : (x + 1) * height]


def gram_pieces(core, own, other):
    rows = own.shape[1]
    vmem = pl.BlockSpec(memory_space=pltpu.VMEM)
    return pl.pallas_call(
        gram_kernel,
        in_specs=[pl.BlockSpec(memory_space=pltpu.SMEM), vmem, vmem],
        out_specs=[vmem, vmem],
        out_shape=[
            jax.ShapeDtypeStruct((RANK, rows), jnp.float32),
            jax.ShapeDtypeStruct((NX, 3 * LANES // (NX * NC), LANES), jnp.float32),
        ],
        compiler_params=pltpu.CompilerParams(vmem_limit_bytes=16 * 2**20),
        cost_estimate=pl.CostEstimate(flops=10**9, bytes_accessed=10**6, transcendentals=0),
        name="gram_pieces",
    )(core.reshape(1), own, other)


def prepare_kernel(core_ref, place_ref, squares_ref, basis_ref, own_ref, left_ref, q_ref):
    rows = left_ref.shape[0] // 2
    half = RANK // NC
    inverse = 1.0 / jnp.sqrt(squares_ref[...] + 1e-06)
    turned = jnp.concatenate([inverse[:, half:], inverse[:, :half]], axis=1)
    inverse = jnp.where(core_ref[0] == 0, inverse, turned)
    basis = jnp.dot(
        own_ranks(core_ref[0], RANK), basis_ref[:, :rows], preferred_element_type=jnp.float32
    ).T
    left_ref[:rows] = basis.astype(jnp.bfloat16)
    left_ref[rows:] = (basis * inverse).astype(jnp.bfloat16)
    rank = lax.broadcasted_iota(jnp.int32, (SUB, half), 1)
    chosen = rank == place_ref[0] + lax.broadcasted_iota(jnp.int32, (SUB, half), 0)
    scale = jnp.sum(jnp.where(chosen, inverse[:, :half], 0.0), axis=1, keepdims=True)
    chosen = jnp.where(chosen, 1.0, 0.0).astype(jnp.bfloat16)
    width = own_ref.shape[2]
    for side in range(2):
        picked = jnp.dot(chosen, own_ref[side], preferred_element_type=jnp.float32) * scale
        columns = slice(side * width, (side + 1) * width)
        q_ref[:, columns] = picked[: q_ref.shape[0]].astype(jnp.bfloat16)


def finish_kernel(
    left_ref,
    own_ref,
    other_ref,
    blended_ref,
    momentum_hbm,
    update_hbm,
    momentum_ref,
    update_ref,
    sems,
):
    rows, cols = blended_ref.shape
    blocks = sems.shape[1]
    width = cols // blocks
    copies = []
    for j in range(blocks):
        columns = slice(j * width, (j + 1) * width)
        side, k = divmod(j, blocks // 2)
        there = slice(k * width, (k + 1) * width)
        project = [ref[side, :, there] for ref in (own_ref, other_ref)]
        project = jnp.concatenate(project, axis=0)
        both = jnp.dot(left_ref[...], project, preferred_element_type=jnp.float32)
        blended = blended_ref[:, columns].astype(jnp.float32)
        momentum = blended - (1.0 - MU_KEEP) * both[:rows]
        momentum_ref[:, columns] = momentum.astype(jnp.bfloat16)
        update_ref[:, columns] = (math.sqrt(D * FF / RANK) * both[rows:]).astype(jnp.bfloat16)
        for n, (source, target) in enumerate(
            ((momentum_ref, momentum_hbm), (update_ref, update_hbm))
        ):
            copy = pltpu.make_async_copy(
                source.at[:, columns], target.at[:, columns], sems.at[n, j]
            )
            copy.start()
            copies.append(copy)
    for copy in copies:
        copy.wait()


def finish(core, place, squares, basis_t, own, other, blended, rank_dev):
    rows, cols = blended.shape
    whole = ((rows, cols), jnp.bfloat16)
    left, q_next = in_vmem(
        prepare_kernel,
        "prepare",
        10**5,
        [((2 * rows, RANK), jnp.bfloat16), ((rank_dev, cols), jnp.bfloat16)],
        core.reshape(1),
        place.reshape(1),
        squares,
        basis_t,
        own,
        scalars=2,
    )
    momentum_next, update = in_vmem(
        finish_kernel,
        "finish",
        4 * rows * RANK * cols,
        [whole, whole],
        left,
        own,
        other,
        blended,
        scratch=[pltpu.VMEM(*whole), pltpu.VMEM(*whole), pltpu.SemaphoreType.DMA((2, BLOCKS))],
        hbm_outs=2,
    )
    return momentum_next, update, q_next


def body(gradient, momentum, q_basis):
    core, x, y = lax.axis_index("c"), lax.axis_index("x"), lax.axis_index("y")
    rank_dev, cols = q_basis.shape
    half = RANK // NC
    blended = (momentum.astype(jnp.float32) + gradient.astype(jnp.float32)).astype(jnp.bfloat16)

    q_own = gather(q_basis, "y", NY).reshape(-1, cols)
    q_own, other = lax.optimization_barrier((q_own, swap_cores(blended)))
    q_own = lax.all_gather(q_own, "x", axis=0, tiled=True)
    rows = NC * blended.shape[0]
    (spread,) = in_vmem(
        power_kernel,
        "power",
        2 * half * rows * cols,
        [((NZ, half, rows), jnp.bfloat16)],
        q_own,
        blended,
        other,
    )
    power_own = jnp.sum(
        lax.all_to_all(spread, "z", 0, 0, tiled=True).astype(jnp.float32), axis=0
    )
    power_t, pieces = gram_pieces(core, power_own, swap_cores(power_own))
    basis_t, terms = orthonormal(core, gram_sum(pieces), power_t, blended, other)

    terms = terms.reshape(NX, NY * SUB, cols // 2)
    project = scatter_sum(terms, "x").astype(jnp.bfloat16).reshape(NY, SUB, cols // 2)
    project = scatter_sum(project, "y").astype(jnp.bfloat16)
    project = gather(project, "y", NY).reshape(NY * SUB, cols // 2)
    peers = NC * NX * NZ
    (spread,) = in_vmem(
        squares_kernel,
        "squares",
        10**6,
        [((peers, 1, NY * SUB), jnp.float32)],
        project,
    )
    squares = lax.all_to_all(spread, ("c", "x", "z"), 0, 0, tiled=True)
    squares = jnp.sum(squares.reshape(NC, 2, NX // 2, NZ, NY * SUB), axis=(1, 3)).reshape(1, RANK)
    project = lax.all_gather(project, "x", axis=0, tiled=True)
    project, squares = lax.optimization_barrier((project, squares))
    project = project.reshape(2, half, cols // 2)
    place = (y * NX + x) * rank_dev
    return finish(
        core, place, squares, basis_t, project, swap_cores(project), blended, rank_dev
    )


def solution(mesh):
    split = Mesh(mesh.devices.reshape(NY, NX, NC, NZ), ("y", "x", "c", "z"))
    spec = P(("y", "x", "c"), "z")
    return jax.shard_map(
        body,
        mesh=split,
        in_specs=(spec, spec, spec),
        out_specs=(spec, spec, spec),
        check_vma=False,
    )
```

```python
import math

import jax
import jax.numpy as jnp
from jax import lax
from jax.experimental import pallas as pl
from jax.experimental.pallas import tpu as pltpu
from jax.sharding import Mesh
from jax.sharding import PartitionSpec as P

D = 8192
FF = 28672
RANK = 256


MU_KEEP = 0.9

NY, NX, NC, NZ = 8, 4, 2, 8


def swap_cores(value):
    return lax.ppermute(value, "c", [(0, 1), (1, 0)])


def gather(value, axis, size):
    spread = jnp.broadcast_to(value[None], (size, *value.shape))
    return lax.all_to_all(spread, axis, 0, 0, tiled=True)


def scatter_sum(value, axis):
    return jnp.sum(lax.all_to_all(value, axis, 0, 0, tiled=True).astype(jnp.float32), axis=0)


def in_vmem(kernel, name, flops, outs, *args, scalars=0, scratch=(), hbm_outs=0):
    vmem, smem, hbm = (pl.BlockSpec(memory_space=m) for m in (pltpu.VMEM, pltpu.SMEM, pl.ANY))
    return pl.pallas_call(
        kernel,
        in_specs=[smem] * scalars + [vmem] * (len(args) - scalars),
        out_specs=[hbm] * hbm_outs + [vmem] * (len(outs) - hbm_outs),
        out_shape=[jax.ShapeDtypeStruct(shape, dtype) for shape, dtype in outs],
        scratch_shapes=list(scratch),
        compiler_params=pltpu.CompilerParams(vmem_limit_bytes=24 * 2**20),
        cost_estimate=pl.CostEstimate(flops=flops, bytes_accessed=10**6, transcendentals=0),
        name=name,
    )(*args)


def power_kernel(core_ref, q_ref, blended_ref, other_ref, spread_ref):
    contract_last = (((1,), (1,)), ((), ()))
    own, other = (
        lax.dot_general(
            q_ref[...], rows[...], contract_last, preferred_element_type=jnp.float32
        )
        for rows in (blended_ref, other_ref)
    )
    first = core_ref[0] == 0
    power = [jnp.where(first, own, other), jnp.where(first, other, own)]
    power = [p.astype(jnp.bfloat16) for p in power]
    for z in range(NZ):
        for c in range(NC):
            spread_ref[z * NC + c] = power[c]


def squares_kernel(project_ref, spread_ref):
    wide = project_ref[...].astype(jnp.float32)
    sums = jnp.sum(wide * wide, axis=1, keepdims=True)
    line = jnp.broadcast_to(sums, (sums.shape[0], LANES)).T[:1]
    spread_ref[...] = jnp.broadcast_to(line[None], spread_ref.shape)


def gram_sum(pieces):
    part = scatter_sum(pieces, ("x", "c"))
    part = jnp.sum(gather(part, "y", NY), axis=0)
    return gather(part, ("c", "x"), NX * NC).reshape(-1, part.shape[-1])


SUB, LANES = 8, 128
PANEL = 64
STEP = 16
BLOCKS = 14


def across(value, lane):
    return jnp.broadcast_to(value[:, lane : lane + 1], (SUB, LANES))


def down(value, row):
    return jnp.broadcast_to(value[row : row + 1, :], (SUB, LANES))


def total(values):
    while len(values) > 1:
        pairs = [values[i] + values[i + 1] for i in range(0, len(values) - 1, 2)]
        values = pairs + values[len(pairs) * 2 :]
    return values[0]


def eliminate(tiles, base, last):
    first = base // LANES
    groups = PANEL // SUB
    depth = STEP // SUB
    row_id = lax.broadcasted_iota(jnp.int32, (SUB, LANES), 0)
    for top in range(0, groups, depth):
        lane = (base + top * SUB) % LANES
        cols = [
            {g: across(tiles[g, first], lane + k) for g in range(top + k // SUB, groups)}
            for k in range(STEP)
        ]
        rows, steps, pivots = [], [], [None] * depth
        for k in range(STEP):
            level, row = divmod(k, SUB)
            here = top + level
            pivot = down(cols[k][here], row)
            inverse = 1.0 / pivot
            known = pivots[level]
            pivots[level] = pivot if known is None else jnp.where(row_id == row, pivot, known)
            step = {g: cols[k][g] * inverse for g in range(here, groups)}
            step[here] = jnp.where(row_id > row, step[here], 0.0)
            for m in range(k + 1, STEP):
                entry = down(cols[k][top + m // SUB], m % SUB)
                for g in cols[m]:
                    cols[m][g] = cols[m][g] - step[g] * entry
            line = {t: down(tiles[here, t], row) for t in range(first, last)}
            for g in range(here, top + depth):
                for t in range(first, last):
                    tiles[g, t] = tiles[g, t] - step[g] * line[t]
            rows.append(line)
            steps.append(step)
        for g in range(top + depth, groups):
            for t in range(first, last):
                tiles[g, t] = tiles[g, t] - total([s[g] * r[t] for s, r in zip(steps, rows)])
        for level in range(depth):
            scale = lax.rsqrt(pivots[level])
            for t in range(first, last):
                tiles[top + level, t] = tiles[top + level, t] * scale


def own_ranks(core, height):
    j = lax.broadcasted_iota(jnp.int32, (height, RANK), 0)
    source = lax.broadcasted_iota(jnp.int32, (height, RANK), 1)
    size = RANK // (NY * NX * NC)
    c = jnp.where(j < RANK // NC, core, 1 - core)
    j = j & (RANK // NC - 1)
    low = j & (size - 1)
    return ((j - low) * NC + c * size + low == source).astype(jnp.bfloat16)


def orthonormal_kernel(
    core_ref,
    gram_ref,
    power_ref,
    other_power_ref,
    blended_ref,
    other_ref,
    basis_ref,
    terms_ref,
    work_ref,
):
    last = work_ref.shape[1] // LANES
    half, core = LANES // 2, LANES * 3 // 2
    work_ref[:LANES, :LANES] = gram_ref[:LANES]
    work_ref[:half, LANES:RANK] = gram_ref[LANES:core]
    work_ref[half:LANES, LANES:RANK] = gram_ref[core + LANES :]
    work_ref[LANES:, LANES:RANK] = gram_ref[core : core + LANES]
    work_ref[:, RANK : RANK + LANES] = power_ref[...]
    work_ref[:, RANK + LANES :] = other_power_ref[...]
    for base in range(0, RANK, PANEL):
        first = base // LANES
        tiles = {
            (g, t): work_ref[base + g * SUB : base + (g + 1) * SUB, t * LANES : (t + 1) * LANES]
            for g in range(PANEL // SUB)
            for t in range(first, last)
        }
        eliminate(tiles, base, last)
        for (g, t), tile in tiles.items():
            work_ref[base + g * SUB : base + (g + 1) * SUB, t * LANES : (t + 1) * LANES] = tile
        below = base + PANEL
        if below < RANK:
            start = below // LANES * LANES
            product = lax.dot_general(
                work_ref[base:below, start:RANK],
                work_ref[base:below, start:],
                (((0,), (0,)), ((), ())),
                precision=lax.Precision.HIGHEST,
                preferred_element_type=jnp.float32,
            )
            work_ref[below:, start:] = work_ref[below:, start:] - product[below - start :]
    basis_ref[...] = work_ref[:, RANK:].astype(basis_ref.dtype)
    mine = jnp.dot(
        own_ranks(core_ref[0], RANK // NC), basis_ref[...], preferred_element_type=jnp.float32
    )
    mine = mine.astype(jnp.bfloat16)
    width = terms_ref.shape[2] // 2
    for j in range(4):
        columns = slice(j * width, (j + 1) * width)
        both = jnp.concatenate([blended_ref[:, columns], other_ref[:, columns]], axis=0)
        terms = jnp.dot(mine, both, preferred_element_type=jnp.float32)
        terms_ref[j // 2, :, j % 2 * width : (j % 2 + 1) * width] = terms.astype(jnp.bfloat16)


def orthonormal(core, gram, power_t, other_power_t, blended, other):
    rows, cols = blended.shape
    vmem = pl.BlockSpec(memory_space=pltpu.VMEM)
    return pl.pallas_call(
        orthonormal_kernel,
        in_specs=[pl.BlockSpec(memory_space=pltpu.SMEM)] + [vmem] * 5,
        out_specs=[vmem, vmem],
        out_shape=[
            jax.ShapeDtypeStruct((RANK, NC * rows), jnp.bfloat16),
            jax.ShapeDtypeStruct((2, RANK // NC, cols // 2), jnp.bfloat16),
        ],
        scratch_shapes=[pltpu.VMEM((RANK, RANK + NC * rows), jnp.float32)],
        compiler_params=pltpu.CompilerParams(vmem_limit_bytes=24 * 2**20),
        cost_estimate=pl.CostEstimate(flops=10**9, bytes_accessed=10**6, transcendentals=0),
        name="orthonormal",
    )(core.reshape(1), gram, power_t, other_power_t, blended, other)


def rank_order(rank_dev):
    def low(value, size):
        return value & (size - 1), value >> (size.bit_length() - 1)

    to = lax.broadcasted_iota(jnp.int32, (RANK, RANK), 0)
    source = lax.broadcasted_iota(jnp.int32, (RANK, RANK), 1)
    i, to = low(to, rank_dev)
    y, to = low(to, NY)
    x, c = low(to, NX)
    return (((y * NX + x) * NC + c) * rank_dev + i == source).astype(jnp.float32)


def gram_kernel(terms_ref, power_ref, gram_ref):
    exact = {"precision": lax.Precision.HIGHEST, "preferred_element_type": jnp.float32}
    halves = [
        total([terms_ref[z * NC + c].astype(jnp.float32) for z in range(NZ)]) for c in range(NC)
    ]
    power = lax.dot_general(
        rank_order(RANK // (NY * NX * NC)),
        jnp.concatenate(halves, axis=0),
        (((0,), (0,)), ((), ())),
        **exact,
    )
    power_ref[...] = power
    contract_last = (((1,), (1,)), ((), ()))
    upper, lower = power[:LANES], power[LANES:]
    top = lax.dot_general(upper, power, contract_last, **exact)
    corner = lax.dot_general(lower, lower, contract_last, **exact)
    cross = top[:, LANES:]
    half = LANES // 2
    gram = jnp.concatenate([top[:, :LANES], cross[:half], corner, cross[half:]], axis=0)
    height = gram_ref.shape[1]
    for x in range(NX):
        for c in range(NC):
            piece = c * NX + x
            gram_ref[x * NC + c] = gram[piece * height : (piece + 1) * height]


def gram_pieces(terms):
    rows = terms.shape[2]
    return in_vmem(
        gram_kernel,
        "gram_pieces",
        10**9,
        [
            ((RANK, rows), jnp.float32),
            ((NX * NC, 3 * LANES // (NX * NC), LANES), jnp.float32),
        ],
        terms,
    )


def prepare_kernel(core_ref, place_ref, squares_ref, basis_ref, own_ref, left_ref, q_ref):
    rows = left_ref.shape[0] // 2
    half = RANK // NC
    inverse = 1.0 / jnp.sqrt(squares_ref[...] + 1e-06)
    turned = jnp.concatenate([inverse[:, half:], inverse[:, :half]], axis=1)
    inverse = jnp.where(core_ref[0] == 0, inverse, turned)
    basis = jnp.dot(
        own_ranks(core_ref[0], RANK), basis_ref[:, :rows], preferred_element_type=jnp.float32
    ).T
    left_ref[:rows] = basis.astype(jnp.bfloat16)
    left_ref[rows:] = (basis * inverse).astype(jnp.bfloat16)
    rank = lax.broadcasted_iota(jnp.int32, (SUB, half), 1)
    chosen = rank == place_ref[0] + lax.broadcasted_iota(jnp.int32, (SUB, half), 0)
    scale = jnp.sum(jnp.where(chosen, inverse[:, :half], 0.0), axis=1, keepdims=True)
    chosen = jnp.where(chosen, 1.0, 0.0).astype(jnp.bfloat16)
    width = own_ref.shape[2]
    for side in range(2):
        picked = jnp.dot(chosen, own_ref[side], preferred_element_type=jnp.float32) * scale
        columns = slice(side * width, (side + 1) * width)
        q_ref[:, columns] = picked[: q_ref.shape[0]].astype(jnp.bfloat16)


def finish_kernel(
    left_ref,
    own_ref,
    other_ref,
    blended_ref,
    momentum_hbm,
    update_hbm,
    momentum_ref,
    update_ref,
    sems,
):
    rows, cols = blended_ref.shape
    blocks = sems.shape[1]
    width = cols // blocks
    copies = []
    for j in range(blocks):
        columns = slice(j * width, (j + 1) * width)
        side, k = divmod(j, blocks // 2)
        there = slice(k * width, (k + 1) * width)
        project = [ref[side, :, there] for ref in (own_ref, other_ref)]
        project = jnp.concatenate(project, axis=0)
        both = jnp.dot(left_ref[...], project, preferred_element_type=jnp.float32)
        blended = blended_ref[:, columns].astype(jnp.float32)
        momentum = blended - (1.0 - MU_KEEP) * both[:rows]
        momentum_ref[:, columns] = momentum.astype(jnp.bfloat16)
        update_ref[:, columns] = (math.sqrt(D * FF / RANK) * both[rows:]).astype(jnp.bfloat16)
        for n, (source, target) in enumerate(
            ((momentum_ref, momentum_hbm), (update_ref, update_hbm))
        ):
            copy = pltpu.make_async_copy(
                source.at[:, columns], target.at[:, columns], sems.at[n, j]
            )
            copy.start()
            copies.append(copy)
    for copy in copies:
        copy.wait()


def finish(core, place, squares, basis_t, own, other, blended, rank_dev):
    rows, cols = blended.shape
    whole = ((rows, cols), jnp.bfloat16)
    left, q_next = in_vmem(
        prepare_kernel,
        "prepare",
        10**5,
        [((2 * rows, RANK), jnp.bfloat16), ((rank_dev, cols), jnp.bfloat16)],
        core.reshape(1),
        place.reshape(1),
        squares,
        basis_t,
        own,
        scalars=2,
    )
    momentum_next, update = in_vmem(
        finish_kernel,
        "finish",
        4 * rows * RANK * cols,
        [whole, whole],
        left,
        own,
        other,
        blended,
        scratch=[pltpu.VMEM(*whole), pltpu.VMEM(*whole), pltpu.SemaphoreType.DMA((2, BLOCKS))],
        hbm_outs=2,
    )
    return momentum_next, update, q_next


def body(gradient, momentum, q_basis):
    core, x, y = lax.axis_index("c"), lax.axis_index("x"), lax.axis_index("y")
    rank_dev, cols = q_basis.shape
    half = RANK // NC
    core, gradient, momentum = lax.optimization_barrier((core, gradient, momentum))
    blended = (momentum.astype(jnp.float32) + gradient.astype(jnp.float32)).astype(jnp.bfloat16)

    q_own = gather(q_basis, "y", NY).reshape(-1, cols)
    q_own, other = lax.optimization_barrier((q_own, swap_cores(blended)))
    q_own = lax.all_gather(q_own, "x", axis=0, tiled=True)
    rows = blended.shape[0]
    (spread,) = in_vmem(
        power_kernel,
        "power",
        4 * half * rows * cols,
        [((NZ * NC, half, rows), jnp.bfloat16)],
        core.reshape(1),
        q_own,
        blended,
        other,
        scalars=1,
    )
    power_t, pieces = gram_pieces(lax.all_to_all(spread, ("z", "c"), 0, 0, tiled=True))
    gram = gram_sum(pieces)
    basis_t, terms = orthonormal(core, gram, power_t, swap_cores(power_t), blended, other)

    terms = terms.reshape(NX, NY * SUB, cols // 2)
    project = scatter_sum(terms, "x").astype(jnp.bfloat16).reshape(NY, SUB, cols // 2)
    project = scatter_sum(project, "y").astype(jnp.bfloat16)
    project = gather(project, "y", NY).reshape(NY * SUB, cols // 2)
    peers = NC * NX * NZ
    (spread,) = in_vmem(
        squares_kernel,
        "squares",
        10**6,
        [((peers, 1, NY * SUB), jnp.float32)],
        project,
    )
    squares = lax.all_to_all(spread, ("c", "x", "z"), 0, 0, tiled=True)
    squares = jnp.sum(squares.reshape(NC, 2, NX // 2, NZ, NY * SUB), axis=(1, 3)).reshape(1, RANK)
    project = lax.all_gather(project, "x", axis=0, tiled=True)
    project, squares = lax.optimization_barrier((project, squares))
    project = project.reshape(2, half, cols // 2)
    place = (y * NX + x) * rank_dev
    return finish(
        core, place, squares, basis_t, project, swap_cores(project), blended, rank_dev
    )


def solution(mesh):
    split = Mesh(mesh.devices.reshape(NY, NX, NC, NZ), ("y", "x", "c", "z"))
    spec = P(("y", "x", "c"), "z")
    return jax.shard_map(
        body,
        mesh=split,
        in_specs=(spec, spec, spec),
        out_specs=(spec, spec, spec),
        check_vma=False,
    )
```

```python
import math

import jax
import jax.numpy as jnp
from jax import lax
from jax.experimental import pallas as pl
from jax.experimental.pallas import tpu as pltpu
from jax.sharding import Mesh
from jax.sharding import PartitionSpec as P

D = 8192
FF = 28672
RANK = 256


MU_KEEP = 0.9

NY, NX, NC, NZ = 8, 4, 2, 8


def swap_cores(value):
    return lax.ppermute(value, "c", [(0, 1), (1, 0)])


def gather(value, axis, size):
    spread = jnp.broadcast_to(value[None], (size, *value.shape))
    return lax.all_to_all(spread, axis, 0, 0, tiled=True)


def scatter_sum(value, axis):
    return jnp.sum(lax.all_to_all(value, axis, 0, 0, tiled=True).astype(jnp.float32), axis=0)


def in_vmem(kernel, name, flops, outs, *args, scalars=0, scratch=(), hbm_outs=0):
    vmem, smem, hbm = (pl.BlockSpec(memory_space=m) for m in (pltpu.VMEM, pltpu.SMEM, pl.ANY))
    return pl.pallas_call(
        kernel,
        in_specs=[smem] * scalars + [vmem] * (len(args) - scalars),
        out_specs=[hbm] * hbm_outs + [vmem] * (len(outs) - hbm_outs),
        out_shape=[jax.ShapeDtypeStruct(shape, dtype) for shape, dtype in outs],
        scratch_shapes=list(scratch),
        compiler_params=pltpu.CompilerParams(vmem_limit_bytes=24 * 2**20),
        cost_estimate=pl.CostEstimate(flops=flops, bytes_accessed=10**6, transcendentals=0),
        name=name,
    )(*args)


def power_kernel(q_ref, blended_ref, other_ref, spread_ref):
    contract_last = (((1,), (1,)), ((), ()))
    power = [
        lax.dot_general(
            q_ref[...], rows[...], contract_last, preferred_element_type=jnp.float32
        ).astype(jnp.bfloat16)
        for rows in (blended_ref, other_ref)
    ]
    power = jnp.concatenate(power, axis=1)
    for z in range(NZ):
        spread_ref[z] = power


def squares_kernel(project_ref, spread_ref):
    wide = project_ref[...].astype(jnp.float32)
    sums = jnp.sum(wide * wide, axis=1, keepdims=True)
    line = jnp.broadcast_to(sums, (sums.shape[0], LANES)).T[:1]
    spread_ref[...] = jnp.broadcast_to(line[None], spread_ref.shape)


def gram_sum(pieces):
    part = scatter_sum(pieces, "x")
    part = jnp.sum(gather(part, "y", NY), axis=0)
    return gather(part, ("c", "x"), NX * NC).reshape(-1, part.shape[-1])


SUB, LANES = 8, 128
PANEL = 64
STEP = 16
BLOCKS = 14


def across(value, lane):
    return jnp.broadcast_to(value[:, lane : lane + 1], (SUB, LANES))


def down(value, row):
    return jnp.broadcast_to(value[row : row + 1, :], (SUB, LANES))


def total(values):
    while len(values) > 1:
        pairs = [values[i] + values[i + 1] for i in range(0, len(values) - 1, 2)]
        values = pairs + values[len(pairs) * 2 :]
    return values[0]


def eliminate(tiles, base, last):
    first = base // LANES
    groups = PANEL // SUB
    depth = STEP // SUB
    row_id = lax.broadcasted_iota(jnp.int32, (SUB, LANES), 0)
    for top in range(0, groups, depth):
        lane = (base + top * SUB) % LANES
        cols = [
            {g: across(tiles[g, first], lane + k) for g in range(top + k // SUB, groups)}
            for k in range(STEP)
        ]
        rows, steps, pivots = [], [], [None] * depth
        for k in range(STEP):
            level, row = divmod(k, SUB)
            here = top + level
            pivot = down(cols[k][here], row)
            inverse = 1.0 / pivot
            known = pivots[level]
            pivots[level] = pivot if known is None else jnp.where(row_id == row, pivot, known)
            step = {g: cols[k][g] * inverse for g in range(here, groups)}
            step[here] = jnp.where(row_id > row, step[here], 0.0)
            for m in range(k + 1, STEP):
                entry = down(cols[k][top + m // SUB], m % SUB)
                for g in cols[m]:
                    cols[m][g] = cols[m][g] - step[g] * entry
            line = {t: down(tiles[here, t], row) for t in range(first, last)}
            for g in range(here, top + depth):
                for t in range(first, last):
                    tiles[g, t] = tiles[g, t] - step[g] * line[t]
            rows.append(line)
            steps.append(step)
        for g in range(top + depth, groups):
            for t in range(first, last):
                tiles[g, t] = tiles[g, t] - total([s[g] * r[t] for s, r in zip(steps, rows)])
        for level in range(depth):
            scale = lax.rsqrt(pivots[level])
            for t in range(first, last):
                tiles[top + level, t] = tiles[top + level, t] * scale


def own_ranks(core, height):
    j = lax.broadcasted_iota(jnp.int32, (height, RANK), 0)
    source = lax.broadcasted_iota(jnp.int32, (height, RANK), 1)
    size = RANK // (NY * NX * NC)
    c = jnp.where(j < RANK // NC, core, 1 - core)
    j = j & (RANK // NC - 1)
    low = j & (size - 1)
    return ((j - low) * NC + c * size + low == source).astype(jnp.bfloat16)


def orthonormal_kernel(
    core_ref, gram_ref, power_ref, blended_ref, other_ref, basis_ref, terms_ref, work_ref
):
    last = work_ref.shape[1] // LANES
    half, core = LANES // 2, LANES * 3 // 2
    work_ref[:LANES, :LANES] = gram_ref[:LANES]
    work_ref[:half, LANES:RANK] = gram_ref[LANES:core]
    work_ref[half:LANES, LANES:RANK] = gram_ref[core + LANES :]
    work_ref[LANES:, LANES:RANK] = gram_ref[core : core + LANES]
    work_ref[:, RANK:] = power_ref[...]
    for base in range(0, RANK, PANEL):
        first = base // LANES
        tiles = {
            (g, t): work_ref[base + g * SUB : base + (g + 1) * SUB, t * LANES : (t + 1) * LANES]
            for g in range(PANEL // SUB)
            for t in range(first, last)
        }
        eliminate(tiles, base, last)
        for (g, t), tile in tiles.items():
            work_ref[base + g * SUB : base + (g + 1) * SUB, t * LANES : (t + 1) * LANES] = tile
        below = base + PANEL
        if below < RANK:
            start = below // LANES * LANES
            product = lax.dot_general(
                work_ref[base:below, start:RANK],
                work_ref[base:below, start:],
                (((0,), (0,)), ((), ())),
                precision=lax.Precision.HIGHEST,
                preferred_element_type=jnp.float32,
            )
            work_ref[below:, start:] = work_ref[below:, start:] - product[below - start :]
    basis_ref[...] = work_ref[:, RANK:].astype(basis_ref.dtype)
    mine = jnp.dot(
        own_ranks(core_ref[0], RANK // NC), basis_ref[...], preferred_element_type=jnp.float32
    )
    mine = mine.astype(jnp.bfloat16)
    width = terms_ref.shape[2] // 2
    for j in range(4):
        columns = slice(j * width, (j + 1) * width)
        both = jnp.concatenate([blended_ref[:, columns], other_ref[:, columns]], axis=0)
        terms = jnp.dot(mine, both, preferred_element_type=jnp.float32)
        terms_ref[j // 2, :, j % 2 * width : (j % 2 + 1) * width] = terms.astype(jnp.bfloat16)


def orthonormal(core, gram, power_t, blended, other):
    rows, cols = blended.shape
    vmem = pl.BlockSpec(memory_space=pltpu.VMEM)
    return pl.pallas_call(
        orthonormal_kernel,
        in_specs=[pl.BlockSpec(memory_space=pltpu.SMEM), vmem, vmem, vmem, vmem],
        out_specs=[vmem, vmem],
        out_shape=[
            jax.ShapeDtypeStruct((RANK, NC * rows), jnp.bfloat16),
            jax.ShapeDtypeStruct((2, RANK // NC, cols // 2), jnp.bfloat16),
        ],
        scratch_shapes=[pltpu.VMEM((RANK, RANK + NC * rows), jnp.float32)],
        compiler_params=pltpu.CompilerParams(vmem_limit_bytes=24 * 2**20),
        cost_estimate=pl.CostEstimate(flops=10**9, bytes_accessed=10**6, transcendentals=0),
        name="orthonormal",
    )(core.reshape(1), gram, power_t, blended, other)


def own_first(core, rank_dev):
    def low(value, size):
        return value & (size - 1), value >> (size.bit_length() - 1)

    to = lax.broadcasted_iota(jnp.int32, (RANK, RANK), 0)
    source = lax.broadcasted_iota(jnp.int32, (RANK, RANK), 1)
    i, to = low(to, rank_dev)
    y, to = low(to, NY)
    x, c = low(to, NX)
    c = (c + core) & (NC - 1)
    return (((y * NX + x) * NC + c) * rank_dev + i == source).astype(jnp.float32)


def gram_kernel(core_ref, own_ref, other_ref, power_ref, gram_ref):
    half = own_ref.shape[1] // 2
    other = jnp.concatenate([other_ref[:, half:], other_ref[:, :half]], axis=1)
    exact = {"precision": lax.Precision.HIGHEST, "preferred_element_type": jnp.float32}
    power = lax.dot_general(
        own_first(core_ref[0], RANK // (NY * NX * NC)),
        jnp.concatenate([own_ref[...], other], axis=0),
        (((0,), (0,)), ((), ())),
        **exact,
    )
    power_ref[...] = power
    first = core_ref[0] == 0
    upper, lower = power[:LANES], power[LANES:]
    own = jnp.where(first, upper, lower)
    cross = jnp.where(first, upper[: LANES // 2], upper[LANES // 2 :])
    contract_last = (((1,), (1,)), ((), ()))
    gram = jnp.concatenate(
        [
            lax.dot_general(own, own, contract_last, **exact),
            lax.dot_general(cross, lower, contract_last, **exact),
        ],
        axis=0,
    )
    height = gram_ref.shape[1]
    for x in range(NX):
        gram_ref[x] = gram[x * height : (x + 1) * height]


def gram_pieces(core, own, other):
    rows = own.shape[1]
    vmem = pl.BlockSpec(memory_space=pltpu.VMEM)
    return pl.pallas_call(
        gram_kernel,
        in_specs=[pl.BlockSpec(memory_space=pltpu.SMEM), vmem, vmem],
        out_specs=[vmem, vmem],
        out_shape=[
            jax.ShapeDtypeStruct((RANK, rows), jnp.float32),
            jax.ShapeDtypeStruct((NX, 3 * LANES // (NX * NC), LANES), jnp.float32),
        ],
        compiler_params=pltpu.CompilerParams(vmem_limit_bytes=16 * 2**20),
        cost_estimate=pl.CostEstimate(flops=10**9, bytes_accessed=10**6, transcendentals=0),
        name="gram_pieces",
    )(core.reshape(1), own, other)


def prepare_kernel(
    core_ref, place_ref, squares_ref, basis_ref, own_ref, blended_ref, left_ref, part_ref, q_ref
):
    rows = blended_ref.shape[0]
    half = RANK // NC
    inverse = 1.0 / jnp.sqrt(squares_ref[...] + 1e-06)
    turned = jnp.concatenate([inverse[:, half:], inverse[:, :half]], axis=1)
    inverse = jnp.where(core_ref[0] == 0, inverse, turned)
    basis = jnp.dot(
        own_ranks(core_ref[0], RANK), basis_ref[:, :rows], preferred_element_type=jnp.float32
    ).T
    left = jnp.concatenate([basis, basis * inverse], axis=0).astype(jnp.bfloat16)
    left_ref[...] = left[:, half:]
    rank = lax.broadcasted_iota(jnp.int32, (SUB, half), 1)
    chosen = rank == place_ref[0] + lax.broadcasted_iota(jnp.int32, (SUB, half), 0)
    scale = jnp.sum(jnp.where(chosen, inverse[:, :half], 0.0), axis=1, keepdims=True)
    chosen = jnp.where(chosen, 1.0, 0.0).astype(jnp.bfloat16)
    width = own_ref.shape[2]
    for side in range(2):
        picked = jnp.dot(chosen, own_ref[side], preferred_element_type=jnp.float32) * scale
        columns = slice(side * width, (side + 1) * width)
        q_ref[:, columns] = picked[: q_ref.shape[0]].astype(jnp.bfloat16)
        both = jnp.dot(left[:, :half], own_ref[side], preferred_element_type=jnp.float32)
        blended = blended_ref[:, columns].astype(jnp.float32)
        part_ref[:rows, columns] = blended - (1.0 - MU_KEEP) * both[:rows]
        part_ref[rows:, columns] = math.sqrt(D * FF / RANK) * both[rows:]


def finish_kernel(
    left_ref,
    part_ref,
    other_ref,
    momentum_hbm,
    update_hbm,
    momentum_ref,
    update_ref,
    sems,
):
    rows, cols = momentum_ref.shape
    blocks = sems.shape[1]
    width = cols // blocks
    copies = []
    for j in range(blocks):
        columns = slice(j * width, (j + 1) * width)
        side, k = divmod(j, blocks // 2)
        there = slice(k * width, (k + 1) * width)
        both = jnp.dot(left_ref[...], other_ref[side, :, there], preferred_element_type=jnp.float32)
        momentum = part_ref[:rows, columns] - (1.0 - MU_KEEP) * both[:rows]
        momentum_ref[:, columns] = momentum.astype(jnp.bfloat16)
        update = part_ref[rows:, columns] + math.sqrt(D * FF / RANK) * both[rows:]
        update_ref[:, columns] = update.astype(jnp.bfloat16)
        for n, (source, target) in enumerate(
            ((momentum_ref, momentum_hbm), (update_ref, update_hbm))
        ):
            copy = pltpu.make_async_copy(
                source.at[:, columns], target.at[:, columns], sems.at[n, j]
            )
            copy.start()
            copies.append(copy)
    for copy in copies:
        copy.wait()


def finish(core, place, squares, basis_t, own, other, blended, rank_dev):
    rows, cols = blended.shape
    whole = ((rows, cols), jnp.bfloat16)
    left, part, q_next = in_vmem(
        prepare_kernel,
        "prepare",
        10**5,
        [
            ((2 * rows, RANK // NC), jnp.bfloat16),
            ((2 * rows, cols), jnp.float32),
            ((rank_dev, cols), jnp.bfloat16),
        ],
        core.reshape(1),
        place.reshape(1),
        squares,
        basis_t,
        own,
        blended,
        scalars=2,
    )
    momentum_next, update = in_vmem(
        finish_kernel,
        "finish",
        4 * rows * RANK * cols,
        [whole, whole],
        left,
        part,
        other,
        scratch=[pltpu.VMEM(*whole), pltpu.VMEM(*whole), pltpu.SemaphoreType.DMA((2, BLOCKS))],
        hbm_outs=2,
    )
    return momentum_next, update, q_next


def body(gradient, momentum, q_basis):
    core, x, y = lax.axis_index("c"), lax.axis_index("x"), lax.axis_index("y")
    rank_dev, cols = q_basis.shape
    half = RANK // NC
    blended = (momentum.astype(jnp.float32) + gradient.astype(jnp.float32)).astype(jnp.bfloat16)

    q_own = gather(q_basis, "y", NY).reshape(-1, cols)
    q_own, other = lax.optimization_barrier((q_own, swap_cores(blended)))
    q_own = lax.all_gather(q_own, "x", axis=0, tiled=True)
    rows = NC * blended.shape[0]
    (spread,) = in_vmem(
        power_kernel,
        "power",
        2 * half * rows * cols,
        [((NZ, half, rows), jnp.bfloat16)],
        q_own,
        blended,
        other,
    )
    power_own = jnp.sum(
        lax.all_to_all(spread, "z", 0, 0, tiled=True).astype(jnp.float32), axis=0
    )
    power_t, pieces = gram_pieces(core, power_own, swap_cores(power_own))
    basis_t, terms = orthonormal(core, gram_sum(pieces), power_t, blended, other)

    terms = terms.reshape(NX, NY * SUB, cols // 2)
    project = scatter_sum(terms, "x").astype(jnp.bfloat16).reshape(NY, SUB, cols // 2)
    project = scatter_sum(project, "y").astype(jnp.bfloat16)
    project = gather(project, "y", NY).reshape(NY * SUB, cols // 2)
    peers = NC * NX * NZ
    (spread,) = in_vmem(
        squares_kernel,
        "squares",
        10**6,
        [((peers, 1, NY * SUB), jnp.float32)],
        project,
    )
    squares = lax.all_to_all(spread, ("c", "x", "z"), 0, 0, tiled=True)
    squares = jnp.sum(squares.reshape(NC, 2, NX // 2, NZ, NY * SUB), axis=(1, 3)).reshape(1, RANK)
    project = lax.all_gather(project, "x", axis=0, tiled=True)
    project, squares = lax.optimization_barrier((project, squares))
    project = project.reshape(2, half, cols // 2)
    place = (y * NX + x) * rank_dev
    return finish(
        core, place, squares, basis_t, project, swap_cores(project), blended, rank_dev
    )


def solution(mesh):
    split = Mesh(mesh.devices.reshape(NY, NX, NC, NZ), ("y", "x", "c", "z"))
    spec = P(("y", "x", "c"), "z")
    return jax.shard_map(
        body,
        mesh=split,
        in_specs=(spec, spec, spec),
        out_specs=(spec, spec, spec),
        check_vma=False,
    )
```

```python
import math

import jax
import jax.numpy as jnp
from jax import lax
from jax.experimental import pallas as pl
from jax.experimental.pallas import tpu as pltpu
from jax.sharding import Mesh
from jax.sharding import PartitionSpec as P

D = 8192
FF = 28672
RANK = 256


MU_KEEP = 0.9

NY, NX, NC, NZ = 8, 4, 2, 8


def swap_cores(value):
    return lax.ppermute(value, "c", [(0, 1), (1, 0)])


def gather(value, axis, size):
    spread = jnp.broadcast_to(value[None], (size, *value.shape))
    return lax.all_to_all(spread, axis, 0, 0, tiled=True)


def scatter_sum(value, axis):
    return jnp.sum(lax.all_to_all(value, axis, 0, 0, tiled=True).astype(jnp.float32), axis=0)


def in_vmem(kernel, name, flops, outs, *args, scalars=0, scratch=(), hbm_outs=0):
    vmem, smem, hbm = (pl.BlockSpec(memory_space=m) for m in (pltpu.VMEM, pltpu.SMEM, pl.ANY))
    return pl.pallas_call(
        kernel,
        in_specs=[smem] * scalars + [vmem] * (len(args) - scalars),
        out_specs=[hbm] * hbm_outs + [vmem] * (len(outs) - hbm_outs),
        out_shape=[jax.ShapeDtypeStruct(shape, dtype) for shape, dtype in outs],
        scratch_shapes=list(scratch),
        compiler_params=pltpu.CompilerParams(vmem_limit_bytes=24 * 2**20),
        cost_estimate=pl.CostEstimate(flops=flops, bytes_accessed=10**6, transcendentals=0),
        name=name,
    )(*args)


def power_kernel(q_ref, blended_ref, other_ref, spread_ref):
    contract_last = (((1,), (1,)), ((), ()))
    power = [
        lax.dot_general(
            q_ref[...], rows[...], contract_last, preferred_element_type=jnp.float32
        ).astype(jnp.bfloat16)
        for rows in (blended_ref, other_ref)
    ]
    power = jnp.concatenate(power, axis=1)
    for z in range(NZ):
        spread_ref[z] = power


def squares_kernel(project_ref, spread_ref):
    wide = project_ref[...].astype(jnp.float32)
    sums = jnp.sum(wide * wide, axis=1, keepdims=True)
    line = jnp.broadcast_to(sums, (sums.shape[0], LANES)).T[:1]
    spread_ref[...] = jnp.broadcast_to(line[None], spread_ref.shape)


def gram_sum(pieces):
    part = scatter_sum(pieces, "x")
    part = jnp.sum(gather(part, "y", NY), axis=0)
    return gather(part, ("c", "x"), NX * NC).reshape(-1, part.shape[-1])


SUB, LANES = 8, 128
PANEL = 64
STEP = 16
BLOCKS = 4


def across(value, lane):
    return jnp.broadcast_to(value[:, lane : lane + 1], (SUB, LANES))


def down(value, row):
    return jnp.broadcast_to(value[row : row + 1, :], (SUB, LANES))


def total(values):
    while len(values) > 1:
        pairs = [values[i] + values[i + 1] for i in range(0, len(values) - 1, 2)]
        values = pairs + values[len(pairs) * 2 :]
    return values[0]


def eliminate(tiles, base, last):
    first = base // LANES
    groups = PANEL // SUB
    depth = STEP // SUB
    row_id = lax.broadcasted_iota(jnp.int32, (SUB, LANES), 0)
    for top in range(0, groups, depth):
        lane = (base + top * SUB) % LANES
        cols = [
            {g: across(tiles[g, first], lane + k) for g in range(top + k // SUB, groups)}
            for k in range(STEP)
        ]
        rows, steps, pivots = [], [], [None] * depth
        for k in range(STEP):
            level, row = divmod(k, SUB)
            here = top + level
            pivot = down(cols[k][here], row)
            inverse = 1.0 / pivot
            known = pivots[level]
            pivots[level] = pivot if known is None else jnp.where(row_id == row, pivot, known)
            step = {g: cols[k][g] * inverse for g in range(here, groups)}
            step[here] = jnp.where(row_id > row, step[here], 0.0)
            for m in range(k + 1, STEP):
                entry = down(cols[k][top + m // SUB], m % SUB)
                for g in cols[m]:
                    cols[m][g] = cols[m][g] - step[g] * entry
            line = {t: down(tiles[here, t], row) for t in range(first, last)}
            for g in range(here, top + depth):
                for t in range(first, last):
                    tiles[g, t] = tiles[g, t] - step[g] * line[t]
            rows.append(line)
            steps.append(step)
        for g in range(top + depth, groups):
            for t in range(first, last):
                tiles[g, t] = tiles[g, t] - total([s[g] * r[t] for s, r in zip(steps, rows)])
        for level in range(depth):
            scale = lax.rsqrt(pivots[level])
            for t in range(first, last):
                tiles[top + level, t] = tiles[top + level, t] * scale


def own_ranks(core, height):
    j = lax.broadcasted_iota(jnp.int32, (height, RANK), 0)
    source = lax.broadcasted_iota(jnp.int32, (height, RANK), 1)
    size = RANK // (NY * NX * NC)
    c = jnp.where(j < RANK // NC, core, 1 - core)
    j = j & (RANK // NC - 1)
    low = j & (size - 1)
    return ((j - low) * NC + c * size + low == source).astype(jnp.bfloat16)


def orthonormal_kernel(
    core_ref, gram_ref, power_ref, blended_ref, other_ref, basis_ref, terms_ref, work_ref
):
    last = work_ref.shape[1] // LANES
    half, core = LANES // 2, LANES * 3 // 2
    work_ref[:LANES, :LANES] = gram_ref[:LANES]
    work_ref[:half, LANES:RANK] = gram_ref[LANES:core]
    work_ref[half:LANES, LANES:RANK] = gram_ref[core + LANES :]
    work_ref[LANES:, LANES:RANK] = gram_ref[core : core + LANES]
    work_ref[:, RANK:] = power_ref[...]
    for base in range(0, RANK, PANEL):
        first = base // LANES
        tiles = {
            (g, t): work_ref[base + g * SUB : base + (g + 1) * SUB, t * LANES : (t + 1) * LANES]
            for g in range(PANEL // SUB)
            for t in range(first, last)
        }
        eliminate(tiles, base, last)
        for (g, t), tile in tiles.items():
            work_ref[base + g * SUB : base + (g + 1) * SUB, t * LANES : (t + 1) * LANES] = tile
        below = base + PANEL
        if below < RANK:
            start = below // LANES * LANES
            product = lax.dot_general(
                work_ref[base:below, start:RANK],
                work_ref[base:below, start:],
                (((0,), (0,)), ((), ())),
                precision=lax.Precision.HIGHEST,
                preferred_element_type=jnp.float32,
            )
            work_ref[below:, start:] = work_ref[below:, start:] - product[below - start :]
    basis_ref[...] = work_ref[:, RANK:].astype(basis_ref.dtype)
    mine = jnp.dot(
        own_ranks(core_ref[0], RANK // NC), basis_ref[...], preferred_element_type=jnp.float32
    )
    mine = mine.astype(jnp.bfloat16)
    width = terms_ref.shape[2] // 2
    for j in range(4):
        columns = slice(j * width, (j + 1) * width)
        both = jnp.concatenate([blended_ref[:, columns], other_ref[:, columns]], axis=0)
        terms = jnp.dot(mine, both, preferred_element_type=jnp.float32)
        terms_ref[j // 2, :, j % 2 * width : (j % 2 + 1) * width] = terms.astype(jnp.bfloat16)


def orthonormal(core, gram, power_t, blended, other):
    rows, cols = blended.shape
    vmem = pl.BlockSpec(memory_space=pltpu.VMEM)
    return pl.pallas_call(
        orthonormal_kernel,
        in_specs=[pl.BlockSpec(memory_space=pltpu.SMEM), vmem, vmem, vmem, vmem],
        out_specs=[vmem, vmem],
        out_shape=[
            jax.ShapeDtypeStruct((RANK, NC * rows), jnp.bfloat16),
            jax.ShapeDtypeStruct((2, RANK // NC, cols // 2), jnp.bfloat16),
        ],
        scratch_shapes=[pltpu.VMEM((RANK, RANK + NC * rows), jnp.float32)],
        compiler_params=pltpu.CompilerParams(vmem_limit_bytes=24 * 2**20),
        cost_estimate=pl.CostEstimate(flops=10**9, bytes_accessed=10**6, transcendentals=0),
        name="orthonormal",
    )(core.reshape(1), gram, power_t, blended, other)


def own_first(core, rank_dev):
    def low(value, size):
        return value & (size - 1), value >> (size.bit_length() - 1)

    to = lax.broadcasted_iota(jnp.int32, (RANK, RANK), 0)
    source = lax.broadcasted_iota(jnp.int32, (RANK, RANK), 1)
    i, to = low(to, rank_dev)
    y, to = low(to, NY)
    x, c = low(to, NX)
    c = (c + core) & (NC - 1)
    return (((y * NX + x) * NC + c) * rank_dev + i == source).astype(jnp.float32)


def gram_kernel(core_ref, own_ref, other_ref, power_ref, gram_ref):
    half = own_ref.shape[1] // 2
    other = jnp.concatenate([other_ref[:, half:], other_ref[:, :half]], axis=1)
    exact = {"precision": lax.Precision.HIGHEST, "preferred_element_type": jnp.float32}
    power = lax.dot_general(
        own_first(core_ref[0], RANK // (NY * NX * NC)),
        jnp.concatenate([own_ref[...], other], axis=0),
        (((0,), (0,)), ((), ())),
        **exact,
    )
    power_ref[...] = power
    first = core_ref[0] == 0
    upper, lower = power[:LANES], power[LANES:]
    own = jnp.where(first, upper, lower)
    cross = jnp.where(first, upper[: LANES // 2], upper[LANES // 2 :])
    contract_last = (((1,), (1,)), ((), ()))
    gram = jnp.concatenate(
        [
            lax.dot_general(own, own, contract_last, **exact),
            lax.dot_general(cross, lower, contract_last, **exact),
        ],
        axis=0,
    )
    height = gram_ref.shape[1]
    for x in range(NX):
        gram_ref[x] = gram[x * height : (x + 1) * height]


def gram_pieces(core, own, other):
    rows = own.shape[1]
    vmem = pl.BlockSpec(memory_space=pltpu.VMEM)
    return pl.pallas_call(
        gram_kernel,
        in_specs=[pl.BlockSpec(memory_space=pltpu.SMEM), vmem, vmem],
        out_specs=[vmem, vmem],
        out_shape=[
            jax.ShapeDtypeStruct((RANK, rows), jnp.float32),
            jax.ShapeDtypeStruct((NX, 3 * LANES // (NX * NC), LANES), jnp.float32),
        ],
        compiler_params=pltpu.CompilerParams(vmem_limit_bytes=16 * 2**20),
        cost_estimate=pl.CostEstimate(flops=10**9, bytes_accessed=10**6, transcendentals=0),
        name="gram_pieces",
    )(core.reshape(1), own, other)


def prepare_kernel(
    core_ref, place_ref, squares_ref, basis_ref, own_ref, blended_ref, left_ref, part_ref, q_ref
):
    rows = blended_ref.shape[0]
    half = RANK // NC
    inverse = 1.0 / jnp.sqrt(squares_ref[...] + 1e-06)
    turned = jnp.concatenate([inverse[:, half:], inverse[:, :half]], axis=1)
    inverse = jnp.where(core_ref[0] == 0, inverse, turned)
    basis = jnp.dot(
        own_ranks(core_ref[0], RANK), basis_ref[:, :rows], preferred_element_type=jnp.float32
    ).T
    left = jnp.concatenate([basis, basis * inverse], axis=0).astype(jnp.bfloat16)
    left_ref[...] = left[:, half:]
    rank = lax.broadcasted_iota(jnp.int32, (SUB, half), 1)
    chosen = rank == place_ref[0] + lax.broadcasted_iota(jnp.int32, (SUB, half), 0)
    scale = jnp.sum(jnp.where(chosen, inverse[:, :half], 0.0), axis=1, keepdims=True)
    chosen = jnp.where(chosen, 1.0, 0.0).astype(jnp.bfloat16)
    width = own_ref.shape[2]
    for side in range(2):
        picked = jnp.dot(chosen, own_ref[side], preferred_element_type=jnp.float32) * scale
        columns = slice(side * width, (side + 1) * width)
        q_ref[:, columns] = picked[: q_ref.shape[0]].astype(jnp.bfloat16)
        both = jnp.dot(left[:, :half], own_ref[side], preferred_element_type=jnp.float32)
        blended = blended_ref[:, columns].astype(jnp.float32)
        part_ref[:rows, columns] = blended - (1.0 - MU_KEEP) * both[:rows]
        part_ref[rows:, columns] = math.sqrt(D * FF / RANK) * both[rows:]


def finish_kernel(
    left_ref,
    part_ref,
    other_ref,
    momentum_hbm,
    update_hbm,
    momentum_ref,
    update_ref,
    sems,
):
    rows, cols = momentum_ref.shape
    blocks = sems.shape[1]
    width = cols // blocks
    copies = []
    for j in range(blocks):
        columns = slice(j * width, (j + 1) * width)
        side, k = divmod(j, blocks // 2)
        there = slice(k * width, (k + 1) * width)
        both = jnp.dot(left_ref[...], other_ref[side, :, there], preferred_element_type=jnp.float32)
        momentum = part_ref[:rows, columns] - (1.0 - MU_KEEP) * both[:rows]
        momentum_ref[:, columns] = momentum.astype(jnp.bfloat16)
        update = part_ref[rows:, columns] + math.sqrt(D * FF / RANK) * both[rows:]
        update_ref[:, columns] = update.astype(jnp.bfloat16)
        for n, (source, target) in enumerate(
            ((momentum_ref, momentum_hbm), (update_ref, update_hbm))
        ):
            copy = pltpu.make_async_copy(
                source.at[:, columns], target.at[:, columns], sems.at[n, j]
            )
            copy.start()
            copies.append(copy)
    for copy in copies:
        copy.wait()


def finish(core, place, squares, basis_t, own, other, blended, rank_dev):
    rows, cols = blended.shape
    whole = ((rows, cols), jnp.bfloat16)
    left, part, q_next = in_vmem(
        prepare_kernel,
        "prepare",
        10**5,
        [
            ((2 * rows, RANK // NC), jnp.bfloat16),
            ((2 * rows, cols), jnp.float32),
            ((rank_dev, cols), jnp.bfloat16),
        ],
        core.reshape(1),
        place.reshape(1),
        squares,
        basis_t,
        own,
        blended,
        scalars=2,
    )
    momentum_next, update = in_vmem(
        finish_kernel,
        "finish",
        4 * rows * RANK * cols,
        [whole, whole],
        left,
        part,
        other,
        scratch=[pltpu.VMEM(*whole), pltpu.VMEM(*whole), pltpu.SemaphoreType.DMA((2, BLOCKS))],
        hbm_outs=2,
    )
    return momentum_next, update, q_next


def body(gradient, momentum, q_basis):
    core, x, y = lax.axis_index("c"), lax.axis_index("x"), lax.axis_index("y")
    rank_dev, cols = q_basis.shape
    half = RANK // NC
    blended = (momentum.astype(jnp.float32) + gradient.astype(jnp.float32)).astype(jnp.bfloat16)

    q_own = gather(q_basis, "y", NY).reshape(-1, cols)
    q_own, other = lax.optimization_barrier((q_own, swap_cores(blended)))
    q_own = lax.all_gather(q_own, "x", axis=0, tiled=True)
    rows = NC * blended.shape[0]
    (spread,) = in_vmem(
        power_kernel,
        "power",
        2 * half * rows * cols,
        [((NZ, half, rows), jnp.bfloat16)],
        q_own,
        blended,
        other,
    )
    power_own = jnp.sum(
        lax.all_to_all(spread, "z", 0, 0, tiled=True).astype(jnp.float32), axis=0
    )
    power_t, pieces = gram_pieces(core, power_own, swap_cores(power_own))
    basis_t, terms = orthonormal(core, gram_sum(pieces), power_t, blended, other)

    terms = terms.reshape(NX, NY * SUB, cols // 2)
    project = scatter_sum(terms, "x").astype(jnp.bfloat16).reshape(NY, SUB, cols // 2)
    project = scatter_sum(project, "y").astype(jnp.bfloat16)
    project = gather(project, "y", NY).reshape(NY * SUB, cols // 2)
    peers = NC * NX * NZ
    (spread,) = in_vmem(
        squares_kernel,
        "squares",
        10**6,
        [((peers, 1, NY * SUB), jnp.float32)],
        project,
    )
    squares = lax.all_to_all(spread, ("c", "x", "z"), 0, 0, tiled=True)
    squares = jnp.sum(squares.reshape(NC, 2, NX // 2, NZ, NY * SUB), axis=(1, 3)).reshape(1, RANK)
    project = lax.all_gather(project, "x", axis=0, tiled=True)
    project, squares = lax.optimization_barrier((project, squares))
    project = project.reshape(2, half, cols // 2)
    place = (y * NX + x) * rank_dev
    return finish(
        core, place, squares, basis_t, project, swap_cores(project), blended, rank_dev
    )


def solution(mesh):
    split = Mesh(mesh.devices.reshape(NY, NX, NC, NZ), ("y", "x", "c", "z"))
    spec = P(("y", "x", "c"), "z")
    return jax.shard_map(
        body,
        mesh=split,
        in_specs=(spec, spec, spec),
        out_specs=(spec, spec, spec),
        check_vma=False,
    )
```
